128 devices in a mesh: dp: 8 (over x_hi, z), tensor: 16 (over x_lo, y, core).
Axes of the slice: x: 4 (x_hi: 2, x_lo: 2; x = x_hi * 2 + x_lo), y: 4, z: 4, core: 2. Of those that a mesh axis runs over, the one named last changes fastest.
Arguments:
- branch_in: bfloat16 [4096, 8192], P('dp', 'tensor'), may hold values from -6 to 6
- gate_in: bfloat16 [4096, 8192], P('dp', 'tensor'), may hold values from -6 to 6
- group_proj: bfloat16 [4096, 4096], P('dp'), may hold values from -6 to 6
- step_raw: bfloat16 [4096, 128], P('dp', 'tensor'), may hold values from -4 to 27
- conv_inner: bfloat16 [4, 8192], P(None, 'tensor'), may hold values from -3 to 3
- conv_groups: bfloat16 [4, 4096], replicated, may hold values from -3 to 3
- step_bias: float32 [128], P('tensor'), may hold values from -2.5 to -1.5
- decay_log: float32 [128], P('tensor'), may hold values from -10 to 0
- skip_gain: float32 [128], P('tensor'), may hold values from 0.5 to 1.5
- norm_gain: float32 [8192], P('tensor'), may hold values from 0.5 to 1.5
- exit_mapping_matrix: bfloat16 [8192, 8192], P('tensor'), may hold values from -0.0625 to 0.0625
- cotangent: bfloat16 [4096, 8192], P(('dp', 'tensor')), may hold values from -6 to 6
Outputs:
- layer_out: bfloat16 [4096, 8192], P(('dp', 'tensor'))
- grad_branch: bfloat16 [4096, 8192], P('dp', 'tensor')
- grad_gate: bfloat16 [4096, 8192], P('dp', 'tensor')
- grad_groups: bfloat16 [4096, 4096], P('dp', 'tensor')
- grad_step: bfloat16 [4096, 128], P('dp', 'tensor')
- grad_outproj: bfloat16 [8192, 8192], P('tensor')
The draws below stay inside these ranges and needn't reach their ends.
All inputs are finite; a program needn't handle non-finite values.
Results may differ from the reference program's by a relative error of at most 0.022.
Values may be sent and summed in bfloat16 or wider, within the bound.
A program may use at most 192 MiB of HBM per device.

```python
import math
import jax
import jax.numpy as jnp
from jax import lax

D = 8192
HEADS = 128
HEAD_DIM = 64
STATE = 256
GROUPS = 8
KERNEL = 4
STRETCH = 128
STRING_LENGTH = 512
SEQS = 8
INNER = 8192
N_TENSOR = 16


def draw_step_raw(key, part):
    key = jax.random.fold_in(key, 11)
    level_key, mark_key = jax.random.split(key)
    row_total = SEQS * STRING_LENGTH
    tier_amounts = 0.5 * jax.random.normal(level_key, (row_total, HEADS), jnp.float32)
    flag_amounts = jax.random.randint(mark_key, (row_total, 1), 0, STRING_LENGTH // 3)
    piece_flurry = jnp.where(flag_amounts == 0, STRING_LENGTH / 24.0 + 2.0, 0.0)
    return (tier_amounts + piece_flurry).astype(jnp.bfloat16)


def draw_decay_log(key, part):
    key = jax.random.fold_in(key, 23)
    slow_key, fast_key, pick_key = jax.random.split(key, 3)
    slow_rate = jnp.exp(jax.random.uniform(slow_key, (HEADS,), jnp.float32, math.log(2.0), math.log(15.0))) / STRING_LENGTH
    fast_rate = jnp.exp(jax.random.uniform(fast_key, (HEADS,), jnp.float32, math.log(0.1), math.log(0.5)))
    share = 0.5
    chosen = jax.random.uniform(pick_key, (HEADS,), jnp.float32) < share
    return jnp.log(jnp.where(chosen, slow_rate, fast_rate))


def levels(key, shape, pieces, least, largest):
    loudness, own = 1.0, jax.random.fold_in(key, 6)
    for position, blocks in pieces:
        draws = jnp.exp(jax.random.uniform(jax.random.fold_in(own, position), (blocks,), jnp.float32, least / len(pieces), largest / len(pieces)))
        loudness = loudness * jnp.repeat(draws, shape[position] // blocks).reshape([-1 if axis == position else 1 for axis in range(len(shape))])
    return loudness


def noise(key, extent, deviation, most, cuts=(), dtype=jnp.bfloat16):
    array = deviation * jax.random.normal(key, extent, jnp.float32)
    if cuts:
        array = array * levels(key, extent, cuts, -0.22, 0.18)
    return jnp.clip(array, -most, most).astype(dtype)


def setup_inputs(seed: int = 0) -> dict:
    streams_of = jax.random.split(jax.random.key(seed), 13)
    branch_in = noise(streams_of[0], (SEQS * STRING_LENGTH, INNER), 1.0, 6.0, ((0, 8), (1, 16)))
    gate_in = noise(streams_of[1], (SEQS * STRING_LENGTH, INNER), 1.0, 6.0, ((0, 8), (1, 16)))
    group_proj = noise(streams_of[2], (SEQS * STRING_LENGTH, 2 * GROUPS * STATE), 1.0, 6.0, ((0, 8),))
    step_raw = draw_step_raw(jax.random.fold_in(streams_of[12], 71), 0)
    conv_inner = noise(streams_of[4], (KERNEL, INNER), 0.5, 3.0, ((1, 16),))
    conv_groups = noise(streams_of[5], (KERNEL, 2 * GROUPS * STATE), 0.5, 3.0)
    step_bias = jnp.clip(-2.5 + 1.0 * jax.random.uniform(streams_of[6], (HEADS,), jnp.float32) ** levels(streams_of[6], (HEADS,), ((0, 16),), -0.2, 0.2), -2.5, -1.5)
    decay_log = draw_decay_log(jax.random.fold_in(streams_of[12], 71), 0)
    skip_gain = jnp.clip(0.5 + 1.0 * jax.random.uniform(streams_of[8], (HEADS,), jnp.float32) ** levels(streams_of[8], (HEADS,), ((0, 16),), -0.2, 0.2), 0.5, 1.5)
    norm_gain = jnp.clip(1.0 + 0.1 * jax.random.normal(streams_of[9], (INNER,), jnp.float32), 0.5, 1.5)
    exit_mapping_matrix = noise(streams_of[10], (INNER, D), INNER ** -0.5, 0.0625, ((0, 16),))
    cotangent = noise(streams_of[11], (SEQS * STRING_LENGTH, D), 1.0, 6.0, ((0, 128),))
    return dict(branch_in=branch_in, gate_in=gate_in, group_proj=group_proj, step_raw=step_raw, conv_inner=conv_inner, conv_groups=conv_groups, step_bias=step_bias, decay_log=decay_log, skip_gain=skip_gain, norm_gain=norm_gain, exit_mapping_matrix=exit_mapping_matrix, cotangent=cotangent)


precise = lax.Precision.HIGHEST
epsilon = 1e-05

def causal_conv(signal, kernel):
    length = signal.shape[0]
    padded = jnp.pad(signal, ((KERNEL - 1, 0), (0, 0)))
    summed = kernel[0] * padded[0:length]
    for offset in range(1, KERNEL):
        summed = summed + kernel[offset] * padded[offset:offset + length]
    return summed

def widened_prefix_pass(values, step_sizes, decay_rates, inputs, readouts):
    length, head_count, head_width = values.shape
    state_width = inputs.shape[2]
    blocks = length // STRETCH
    value_blocks = values.reshape(blocks, STRETCH, head_count, head_width)
    input_blocks = inputs.reshape(blocks, STRETCH, head_count, state_width)
    readout_blocks = readouts.reshape(blocks, STRETCH, head_count, state_width)
    step_blocks = jnp.transpose(step_sizes.reshape(blocks, STRETCH, head_count), (0, 2, 1))
    log_decays = jnp.cumsum(step_blocks * decay_rates[None, :, None], axis=2)
    row_ids = lax.broadcasted_iota(jnp.int32, (STRETCH, STRETCH), 0)
    col_ids = lax.broadcasted_iota(jnp.int32, (STRETCH, STRETCH), 1)
    causal = col_ids <= row_ids
    spread = log_decays[:, :, :, None] - log_decays[:, :, None, :]
    decays = jnp.where(causal, jnp.exp(jnp.where(causal, spread, 0.0)), 0.0)
    scores = jnp.einsum('kihn,kjhn->khij', readout_blocks, input_blocks, precision=precise)
    scores = scores * decays * step_blocks[:, :, None, :]
    within = jnp.einsum('khij,kjhp->kihp', scores, value_blocks, precision=precise)
    final_logs = log_decays[:, :, -1]
    carried_state = jnp.exp(final_logs[:, :, None] - log_decays) * step_blocks
    fresh_states = jnp.einsum('kjhn,khj,kjhp->khnp', input_blocks, carried_state, value_blocks, precision=precise)

    def advance(state_now, stretch_item):
        fade_log, fresh_state = stretch_item
        return (jnp.exp(fade_log)[:, None, None] * state_now + fresh_state, state_now)
    initial = jnp.zeros((head_count, state_width, head_width), jnp.float32)
    previous = lax.scan(advance, initial, (final_logs, fresh_states))[1]
    entering = jnp.transpose(jnp.exp(log_decays), (0, 2, 1))[:, :, :, None]
    across = jnp.einsum('kihn,khnp->kihp', readout_blocks, previous, precision=precise) * entering
    return (within + across).reshape(length, head_count, head_width)

def ssm_mixer(branch_in, gate_in, input_pre, prior_emission, step_raw, conv_inner, conv_input, conv_readout, step_bias, decay_log, skip_gain):
    length = branch_in.shape[0]
    head_count = step_raw.shape[1]
    group_count = input_pre.shape[1] // STATE
    values = jax.nn.silu(causal_conv(branch_in.astype(jnp.float32), conv_inner.astype(jnp.float32)))
    values = values.reshape(length, head_count, HEAD_DIM)
    inputs = jax.nn.silu(causal_conv(input_pre, conv_input.astype(jnp.float32))).reshape(length, group_count, STATE)
    readouts = jax.nn.silu(causal_conv(prior_emission, conv_readout.astype(jnp.float32))).reshape(length, group_count, STATE)
    inputs = jnp.repeat(inputs, head_count // group_count, axis=1)
    readouts = jnp.repeat(readouts, head_count // group_count, axis=1)
    step_sizes = jax.nn.softplus(step_raw.astype(jnp.float32) + step_bias)
    decay_rates = -jnp.exp(decay_log)
    outputs = widened_prefix_pass(values, step_sizes, decay_rates, inputs, readouts) + skip_gain[None, :, None] * values
    return outputs.reshape(length, head_count * HEAD_DIM) * jax.nn.silu(gate_in.astype(jnp.float32))

def reference(branch_in, gate_in, group_proj, step_raw, conv_inner, conv_groups, step_bias, decay_log, skip_gain, norm_gain, exit_mapping_matrix, cotangent):
    group_columns = GROUPS * STATE
    group_span = INNER // GROUPS
    block_width = INNER // N_TENSOR

    def one_sequence(weight_sum, items):
        branch_seq, gate_seq, proj_seq, step_seq, upstream = items

        def local_map(branch_part, gate_part, input_part, readout_part, step_part):
            return ssm_mixer(branch_part, gate_part, input_part, readout_part, step_part, conv_inner, conv_groups[:, :group_columns], conv_groups[:, group_columns:], step_bias, decay_log, skip_gain)
        proj_float = proj_seq.astype(jnp.float32)
        gated_out, pullback = jax.vjp(local_map, branch_seq, gate_seq, proj_float[:, :group_columns], proj_float[:, group_columns:], step_seq)
        squares = lax.optimization_barrier(jnp.sum((gated_out * gated_out).reshape(STRING_LENGTH, GROUPS, group_span), axis=2))
        inv_rms = lax.rsqrt(squares / group_span + epsilon)
        inv_full = jnp.repeat(inv_rms, group_span, axis=1)
        normed = (gated_out * inv_full * norm_gain).astype(jnp.bfloat16)
        layer_sum = jnp.zeros((STRING_LENGTH, D), jnp.float32)
        for part_id in range(N_TENSOR):
            partial_term = jnp.dot(normed[:, part_id * block_width:(part_id + 1) * block_width], exit_mapping_matrix[part_id * block_width:(part_id + 1) * block_width], preferred_element_type=jnp.float32)
            layer_sum = layer_sum + lax.optimization_barrier(partial_term.astype(jnp.bfloat16)).astype(jnp.float32)
        grad_normed = lax.dot_general(upstream, exit_mapping_matrix, (((1,), (1,)), ((), ())), preferred_element_type=jnp.float32)
        weight_part = lax.dot_general(normed, upstream, (((0,), (0,)), ((), ())), preferred_element_type=jnp.float32)
        scaled = norm_gain * grad_normed
        within = lax.optimization_barrier(jnp.sum((gated_out * scaled).reshape(STRING_LENGTH, GROUPS, group_span), axis=2))
        grad_gated = inv_full * scaled - gated_out * jnp.repeat(inv_rms ** 3 * within / group_span, group_span, axis=1)
        grad_branch, grad_gate, derivative_entries, grad_readouts, grad_step = pullback(grad_gated)
        weight_sum = weight_sum + lax.optimization_barrier(weight_part.astype(jnp.bfloat16)).astype(jnp.float32)
        grad_groups = jnp.concatenate([derivative_entries, grad_readouts], axis=1).astype(jnp.bfloat16)
        return (weight_sum, (layer_sum.astype(jnp.bfloat16), grad_branch, grad_gate, grad_groups, grad_step))
    stacked = (branch_in.reshape(SEQS, STRING_LENGTH, INNER), gate_in.reshape(SEQS, STRING_LENGTH, INNER), group_proj.reshape(SEQS, STRING_LENGTH, 2 * group_columns), step_raw.reshape(SEQS, STRING_LENGTH, HEADS), cotangent.reshape(SEQS, STRING_LENGTH, D))
    weight_sum, result_list = lax.scan(one_sequence, jnp.zeros((INNER, D), jnp.float32), stacked)
    layer_out, grad_branch, grad_gate, grad_groups, grad_step = result_list
    return (layer_out.reshape(SEQS * STRING_LENGTH, D), grad_branch.reshape(SEQS * STRING_LENGTH, INNER), grad_gate.reshape(SEQS * STRING_LENGTH, INNER), grad_groups.reshape(SEQS * STRING_LENGTH, 2 * group_columns), grad_step.reshape(SEQS * STRING_LENGTH, HEADS), weight_sum.astype(jnp.bfloat16))
```

```python
import functools
import jax
import jax.numpy as jnp
from jax import lax
from jax.experimental import pallas as pl
from jax.experimental.pallas import tpu as pltpu
from jax.sharding import PartitionSpec as P

HEADS = 128
HEAD_DIM = 64
STATE = 256
GROUPS = 8
KERNEL = 4
STRETCH = 128
LANES = 128
f32, bf16 = jnp.float32, jnp.bfloat16
epsilon = 1e-05
NN = (((1,), (0,)), ((), ()))
NT = (((1,), (1,)), ((), ()))
TN = (((0,), (0,)), ((), ()))


def mm(a, b, dims=NN):
    return lax.dot_general(a, b, dims, preferred_element_type=f32)


def mm_exact(a, b, dims=NN):
    return lax.dot_general(a, b, dims, precision=lax.Precision.HIGHEST, preferred_element_type=f32)


def iota(shape, axis):
    return lax.broadcasted_iota(jnp.int32, shape, axis)


def sigmoid(x):
    return 1.0 / (1.0 + jnp.exp(-x))


def later(x, steps):
    return jnp.where(iota(x.shape, 0) >= steps, pltpu.roll(x, steps, 0), 0.0)


def earlier(x, steps):
    length = x.shape[0]
    return jnp.where(iota(x.shape, 0) < length - steps, pltpu.roll(x, length - steps, 0), 0.0)


def conv(x, taps):
    total = taps[KERNEL - 1 : KERNEL] * x
    for steps in range(1, KERNEL):
        total = total + taps[KERNEL - 1 - steps : KERNEL - steps] * later(x, steps)
    return total


def conv_back(g, taps):
    total = taps[KERNEL - 1 : KERNEL] * g
    for steps in range(1, KERNEL):
        total = total + taps[KERNEL - 1 - steps : KERNEL - steps] * earlier(g, steps)
    return total


def silu_slope(x):
    s = sigmoid(x)
    return s * (1.0 + x * (1.0 - s))


def panels(width):
    return [slice(c, c + LANES) for c in range(0, width, LANES)]


def prepare(r):
    length, channels = r["branch"].shape
    heads = r["step"].shape[1]
    for cols in panels(channels):
        pre = conv(r["branch"][:, cols].astype(f32), r["conv_inner"][:, cols].astype(f32))
        r["v"][:, cols] = pre * sigmoid(pre)
    for source, taps, to in (("in", "conv_in", "i"), ("ro", "conv_ro", "r")):
        for cols in panels(STATE):
            pre = conv(r[source][:, cols].astype(f32), r[taps][:, cols].astype(f32))
            r[to][:, cols] = pre * sigmoid(pre)
    small = r["small"]
    small[...] = jnp.zeros_like(small)
    small[0:1, 0:heads] = r["step_bias"][...]
    small[1:2, 0:heads] = -jnp.exp(r["decay_log"][...])
    small[2:3, 0:heads] = r["skip"][...]
    r["z"][...] = jnp.zeros_like(r["z"])
    r["z"][:, 0:heads] = r["step"][...].astype(f32)
    z = r["z"][...] + small[0:1]
    r["z"][...] = z
    dt = jnp.maximum(z, 0.0) + jnp.log1p(jnp.exp(-jnp.abs(z)))
    r["dt"][...] = dt
    square = (STRETCH, STRETCH)
    below = (iota(square, 1) <= iota(square, 0)).astype(f32)
    for k in range(length // STRETCH):
        rows = slice(k * STRETCH, (k + 1) * STRETCH)
        ld = mm_exact(below, dt[rows] * small[1:2])
        r["ld"][rows] = ld
        r["ldt"][k] = jnp.transpose(ld)[0:8]


def widen(columns, pair):
    first, second = columns[:, 2 * pair : 2 * pair + 1], columns[:, 2 * pair + 1 : 2 * pair + 2]
    low = iota((1, LANES), 1) < HEAD_DIM
    return jnp.where(low, first, second)


def widen_all(row, pairs):
    return jnp.concatenate([widen(row, p) for p in range(pairs)], axis=1)


def split_pair(x):
    low = iota(x.shape, 1) < HEAD_DIM
    zero = jnp.zeros_like(x)
    return jnp.concatenate([jnp.where(low, x, zero), jnp.where(low, zero, x)], axis=0)


def decay_of(ld, ldt, head):
    square = (STRETCH, STRETCH)
    causal = iota(square, 1) <= iota(square, 0)
    spread = ld[:, head : head + 1] - ldt[head : head + 1]
    return jnp.exp(jnp.where(causal, spread, -1e30))


def ssm_forward(r):
    length, channels = r["branch"].shape
    pairs = channels // LANES
    prepare(r)
    small = r["small"]
    state = None
    for k in range(length // STRETCH):
        rows = slice(k * STRETCH, (k + 1) * STRETCH)
        i_wide, r_wide = r["i"][rows], r["r"][rows]
        i_now, r_now = i_wide.astype(bf16), r_wide.astype(bf16)
        ld, ldt, dt = r["ld"][rows], r["ldt"][k], r["dt"][rows]
        scores = mm_exact(r_wide, i_wide, NT)
        enter = jnp.exp(ld)
        last = ld[STRETCH - 1 : STRETCH]
        leave = jnp.exp(last - ld)
        held = jnp.zeros((STATE, channels), bf16) if state is None else state.astype(bf16)
        r["sprev"][k] = held
        across = None if state is None else mm(r_now, held)
        carried = []
        squares = jnp.zeros((STRETCH, 1), f32)
        for p in range(pairs):
            cols = slice(p * LANES, (p + 1) * LANES)
            value = r["v"][rows, cols]
            stepped = widen(dt, p) * value
            weights = jnp.concatenate(
                [(scores * decay_of(ld, ldt, 2 * p + h)).astype(bf16) for h in range(2)], axis=1
            )
            y = mm(weights, split_pair(stepped.astype(bf16)))
            if across is not None:
                y = y + widen(enter, p) * across[:, cols]
            y = y + widen(small[2:3], p) * value
            r["y"][rows, cols] = y
            gate = r["gate"][rows, cols].astype(f32)
            gated = y * (gate * sigmoid(gate))
            r["gated"][rows, cols] = gated
            squares = squares + jnp.sum(gated * gated, axis=1, keepdims=True)
            carried.append((widen(leave, p) * stepped).astype(bf16))
        r["squares"][rows] = squares
        fresh = mm(i_now, jnp.concatenate(carried, axis=1), TN)
        state = fresh if state is None else widen_all(jnp.exp(last), pairs) * state + fresh


def ssm_backward(r):
    length, channels = r["branch"].shape
    heads = r["step"].shape[1]
    pairs = channels // LANES
    prepare(r)
    small = r["small"]
    square = (STRETCH, STRETCH)
    row, col = iota(square, 0), iota(square, 1)
    before = (row < col).astype(bf16)
    before32 = (row < col).astype(f32)
    since32 = (row >= col).astype(f32)
    own = (iota((8, channels), 1) // HEAD_DIM == iota((8, channels), 0)).astype(bf16)
    grad_state = None
    for k in reversed(range(length // STRETCH)):
        rows = slice(k * STRETCH, (k + 1) * STRETCH)
        i_wide, r_wide = r["i"][rows], r["r"][rows]
        i_now, r_now = i_wide.astype(bf16), r_wide.astype(bf16)
        ld, ldt, dt = r["ld"][rows], r["ldt"][k], r["dt"][rows]
        scores = mm_exact(r_wide, i_wide, NT)
        enter = jnp.exp(ld)
        last = ld[STRETCH - 1 : STRETCH]
        leave = jnp.exp(last - ld)
        held = r["sprev"][k]
        across = mm(r_now, held)
        entering, leaving, crossed, direct, left = [], [], [], [], []
        grad_after = None if grad_state is None else grad_state.astype(bf16)
        from_state = None if grad_state is None else mm(i_now, grad_after)
        grad_scores = jnp.zeros(square, f32)
        straddle = []
        for p in range(pairs):
            cols = slice(p * LANES, (p + 1) * LANES)
            value = r["v"][rows, cols]
            dt_wide = widen(dt, p)
            stepped = dt_wide * value
            gate = r["gate"][rows, cols].astype(f32)
            gg = r["gg"][rows, cols]
            r["grad_gate"][rows, cols] = (gg * r["y"][rows, cols] * silu_slope(gate)).astype(bf16)
            gy = gg * (gate * sigmoid(gate))
            gys = split_pair(gy.astype(bf16))
            grad_weights = mm(gys, stepped.astype(bf16), NT)
            weights = []
            for h in range(2):
                decay = decay_of(ld, ldt, 2 * p + h)
                weight = scores * decay
                weights.append(weight.astype(bf16))
                grad_weight = grad_weights[h * STRETCH : (h + 1) * STRETCH]
                grad_scores = grad_scores + grad_weight * decay
                crossing = mm((grad_weight * weight).astype(bf16), before)
                straddle.append(
                    jnp.sum(jnp.where(row >= col, crossing, 0.0), axis=0, keepdims=True)
                )
            grad_stepped = mm(jnp.concatenate(weights, axis=0), gys, TN)
            wide_enter = widen(enter, p) * gy
            entering.append(wide_enter.astype(bf16))
            crossed.append((wide_enter * across[:, cols]).astype(bf16))
            if from_state is not None:
                wide_leave = widen(leave, p)
                back = wide_leave * from_state[:, cols]
                grad_stepped = grad_stepped + back
                left.append((back * stepped).astype(bf16))
                leaving.append((wide_leave * stepped).astype(bf16))
            direct.append((grad_stepped * value).astype(bf16))
            r["gv"][rows, cols] = dt_wide * grad_stepped + widen(small[2:3], p) * gy
        entering = jnp.concatenate(entering, axis=1)
        gs = grad_scores.astype(bf16)
        r["gr"][rows] = mm(gs, i_now) + mm(entering, held, NT)
        grad_in = mm(gs, r_now, TN)
        if grad_after is not None:
            grad_in = grad_in + mm(jnp.concatenate(leaving, axis=1), grad_after, NT)
        r["gi"][rows] = grad_in
        to_heads = lambda parts: mm(own, jnp.concatenate(parts, axis=1), NT)
        grad_x = jnp.concatenate(straddle, axis=0)
        grad_x = grad_x + mm_exact(to_heads(crossed), since32)
        if grad_state is not None:
            grad_x = grad_x + mm_exact(to_heads(left), before32)
            faded = widen_all(jnp.exp(last), pairs) * grad_state
            kept = jnp.sum(faded * held.astype(f32), axis=0, keepdims=True)
            grad_x = grad_x + jnp.sum(own.astype(f32) * kept, axis=1, keepdims=True)
        r["z8"][0:8] = grad_x
        r["z8"][8:16] = to_heads(direct)
        turned = jnp.transpose(r["z8"][...])
        grad_dt = turned[:, 8:16] + turned[:, 0:8] * small[1:2, 0:8]
        r["grad_step"][rows] = (grad_dt * sigmoid(r["z"][rows, 0:8]))[:, 0:heads].astype(bf16)
        grad_state_now = mm(r_now, entering, TN)
        grad_state = grad_state_now if grad_state is None else faded + grad_state_now
    for cols in panels(channels):
        taps = r["conv_inner"][:, cols].astype(f32)
        pre = conv(r["branch"][:, cols].astype(f32), taps)
        r["grad_branch"][:, cols] = conv_back(r["gv"][:, cols] * silu_slope(pre), taps).astype(bf16)
    for source, tap_name, grad in (("in", "conv_in", "gi"), ("ro", "conv_ro", "gr")):
        for cols in panels(STATE):
            taps = r[tap_name][:, cols].astype(f32)
            pre = conv(r[source][:, cols].astype(f32), taps)
            r[grad][:, cols] = conv_back(r[grad][:, cols] * silu_slope(pre), taps)


def shape(dims, dtype):
    return jax.ShapeDtypeStruct(dims, dtype)


NAMES = ["branch", "gate", "in", "ro", "step", "conv_inner", "conv_in", "conv_ro"]
NAMES += ["step_bias", "decay_log", "skip"]


def common_scratch(length, channels):
    return dict(
        v=pltpu.VMEM((length, channels), f32),
        i=pltpu.VMEM((length, STATE), f32),
        r=pltpu.VMEM((length, STATE), f32),
        z=pltpu.VMEM((length, LANES), f32),
        dt=pltpu.VMEM((length, LANES), f32),
        ld=pltpu.VMEM((length, LANES), f32),
        ldt=pltpu.VMEM((length // STRETCH, 8, LANES), f32),
        small=pltpu.VMEM((8, LANES), f32),
    )


def whole(dims):
    return pl.BlockSpec(dims, lambda step, group: (0,) * len(dims))


def group_block(rows, offset):
    return pl.BlockSpec((rows, STATE), lambda step, group: (0, offset + group[0]))


def call(body, group, inputs, extra, outs, scratch):
    length = inputs[0].shape[0]
    args = list(inputs) + list(extra)
    specs = []
    for index, arg in enumerate(args):
        if index in (2, 3):
            specs.append(group_block(length, GROUPS * (index - 2)))
        elif index in (6, 7):
            specs.append(group_block(KERNEL, GROUPS * (index - 6)))
        else:
            specs.append(whole(arg.shape))
    return pl.pallas_call(
        body,
        grid_spec=pltpu.PrefetchScalarGridSpec(
            num_scalar_prefetch=1,
            grid=(1,),
            in_specs=specs,
            out_specs=[whole(out.shape) for out in outs],
            scratch_shapes=scratch,
        ),
        out_shape=outs,
        compiler_params=pltpu.CompilerParams(vmem_limit_bytes=48 * 2**20),
    )(group, *args)


def forward_kernel(group, *refs):
    names = NAMES + ["y", "gated", "squares", "sprev"] + list(common_scratch(512, 512))
    ssm_forward(dict(zip(names, refs)))


def backward_kernel(group, *refs):
    names = NAMES + ["y", "sprev", "grad_normed", "inv_rms", "within", "norm_gain"]
    names += ["grad_branch", "grad_gate", "gi", "gr", "grad_step"]
    names += list(common_scratch(512, 512)) + ["gv", "z8", "gg"]
    r = dict(zip(names, refs))
    inv_rms = r["inv_rms"][...]
    shared = inv_rms * inv_rms * inv_rms * r["within"][...] * (1.0 / (HEADS * HEAD_DIM // GROUPS))
    for cols in panels(r["branch"].shape[1]):
        gate = r["gate"][:, cols].astype(f32)
        gated = r["y"][:, cols] * (gate * sigmoid(gate))
        scaled = r["norm_gain"][:, cols] * r["grad_normed"][:, cols]
        r["gg"][:, cols] = inv_rms * scaled - gated * shared
    r["z8"][...] = jnp.zeros_like(r["z8"])
    ssm_backward(r)


def swap_cores(x):
    size = lax.axis_size("tensor")
    return lax.ppermute(x, "tensor", [(i, i ^ 1) for i in range(size)])


def local(
    branch_in,
    gate_in,
    group_proj,
    step_raw,
    conv_inner,
    conv_groups,
    step_bias,
    decay_log,
    skip_gain,
    norm_gain,
    exit_mapping_matrix,
    cotangent,
):
    length, channels = branch_in.shape
    heads = step_raw.shape[1]
    group_span = HEADS * HEAD_DIM // GROUPS
    place = lax.axis_index("tensor")
    group = (place * heads // (HEADS // GROUPS)).astype(jnp.int32)[None]
    inputs = [branch_in, gate_in, group_proj, group_proj, step_raw, conv_inner, conv_groups]
    inputs += [conv_groups, step_bias[None], decay_log[None], skip_gain[None]]
    full_cotangent = lax.all_gather(cotangent, "tensor", axis=0, tiled=True)
    scratch = common_scratch(length, channels)
    y, gated_out, squares, sprev = call(
        forward_kernel,
        group,
        inputs,
        [],
        [
            shape((length, channels), f32),
            shape((length, channels), f32),
            shape((length, 1), f32),
            shape((length // STRETCH, STATE, channels), bf16),
        ],
        list(scratch.values()),
    )
    inv_rms = lax.rsqrt((squares + swap_cores(squares)) / group_span + epsilon)
    normed = (gated_out * inv_rms * norm_gain).astype(bf16)
    weight_part = lax.dot_general(normed, full_cotangent, TN, preferred_element_type=f32)
    weight_total = lax.psum(weight_part.astype(bf16), "dp")
    layer_part = jnp.dot(normed, exit_mapping_matrix, preferred_element_type=f32).astype(bf16)
    layer_out = lax.psum_scatter(layer_part, "tensor", scatter_dimension=0, tiled=True)
    grad_normed = lax.dot_general(
        full_cotangent, exit_mapping_matrix, NT, preferred_element_type=f32
    )
    within = jnp.sum(gated_out * (norm_gain * grad_normed), axis=1, keepdims=True)
    within = within + swap_cores(within)
    extra = [y, sprev, grad_normed, inv_rms, within, norm_gain[None]]
    scratch.update(
        gv=pltpu.VMEM((length, channels), f32),
        z8=pltpu.VMEM((LANES, LANES), f32),
        gg=pltpu.VMEM((length, channels), f32),
    )
    grad_branch, grad_gate, grad_in, grad_ro, grad_step = call(
        backward_kernel,
        group,
        inputs,
        extra,
        [
            shape((length, channels), bf16),
            shape((length, channels), bf16),
            shape((length, STATE), f32),
            shape((length, STATE), f32),
            shape((length, heads), bf16),
        ],
        list(scratch.values()),
    )
    odd = place % 2 == 1
    total = jnp.where(odd, grad_ro, grad_in) + swap_cores(jnp.where(odd, grad_in, grad_ro))
    size = lax.axis_size("tensor")
    moves = [(i, i // 2 + (i % 2) * (size // 2)) for i in range(size)]
    grad_groups = lax.ppermute(total.astype(bf16), "tensor", moves)
    return layer_out, grad_branch, grad_gate, grad_groups, grad_step, weight_total


def solution(mesh):
    placed = (
        P("dp", "tensor"),
        P("dp", "tensor"),
        P("dp", None),
        P("dp", "tensor"),
        P(None, "tensor"),
        P(),
        P("tensor"),
        P("tensor"),
        P("tensor"),
        P("tensor"),
        P("tensor", None),
        P(("dp", "tensor"), None),
    )
    return jax.shard_map(
        local,
        mesh=mesh,
        in_specs=placed,
        out_specs=(
            P(("dp", "tensor"), None),
            P("dp", "tensor"),
            P("dp", "tensor"),
            P("dp", "tensor"),
            P("dp", "tensor"),
            P("tensor", None),
        ),
        check_vma=False,
    )
```

```python
import functools
from types import SimpleNamespace

import jax
import jax.numpy as jnp
from jax import lax
from jax.experimental import pallas as pl
from jax.experimental.pallas import tpu as pltpu
from jax.sharding import PartitionSpec as P

HEADS = 128
HEAD_DIM = 64
STATE = 256
GROUPS = 8
KERNEL = 4
STRETCH = 128
LANES = 128
f32, bf16 = jnp.float32, jnp.bfloat16
epsilon = 1e-05
NN = (((1,), (0,)), ((), ()))
NT = (((1,), (1,)), ((), ()))
TN = (((0,), (0,)), ((), ()))


def mm(a, b, dims=NN):
    return lax.dot_general(a, b, dims, preferred_element_type=f32)


def mm_exact(a, b, dims=NN):
    return lax.dot_general(a, b, dims, precision=lax.Precision.HIGHEST, preferred_element_type=f32)


def iota(shape, axis):
    return lax.broadcasted_iota(jnp.int32, shape, axis)


def sigmoid(x):
    return 1.0 / (1.0 + jnp.exp(-x))


def later(x, steps):
    return jnp.where(iota(x.shape, 0) >= steps, pltpu.roll(x, steps, 0), 0.0)


def earlier(x, steps):
    length = x.shape[0]
    return jnp.where(iota(x.shape, 0) < length - steps, pltpu.roll(x, length - steps, 0), 0.0)


def conv(x, taps):
    total = taps[KERNEL - 1 : KERNEL] * x
    for steps in range(1, KERNEL):
        total = total + taps[KERNEL - 1 - steps : KERNEL - steps] * later(x, steps)
    return total


def conv_back(g, taps):
    total = taps[KERNEL - 1 : KERNEL] * g
    for steps in range(1, KERNEL):
        total = total + taps[KERNEL - 1 - steps : KERNEL - steps] * earlier(g, steps)
    return total


def silu_slope(x):
    s = sigmoid(x)
    return s * (1.0 + x * (1.0 - s))


def panels(width):
    return [slice(c, c + LANES) for c in range(0, width, LANES)]


def group_taps(r, first, cols):
    start = (first + r.group) * STATE + cols.start
    return r.conv_groups[:, pl.ds(pl.multiple_of(start, LANES), LANES)].astype(f32)


def prepare(r):
    length, channels = r.branch.shape
    heads = r.step.shape[0]
    for cols in panels(channels):
        pre = conv(r.branch[:, cols].astype(f32), r.conv_inner[:, cols].astype(f32))
        r.v[:, cols] = pre * sigmoid(pre)
    for source, first, to in ((r.inp, 0, r.i), (r.ro, GROUPS, r.r)):
        for cols in panels(STATE):
            pre = conv(source[:, cols].astype(f32), group_taps(r, first, cols))
            to[:, cols] = pre * sigmoid(pre)
    small = r.small
    small[...] = jnp.zeros_like(small)
    small[0:1, 0:heads] = r.step_bias[...]
    small[1:2, 0:heads] = -jnp.exp(r.decay_log[...])
    small[2:3, 0:heads] = r.skip[...]
    r.turn[...] = jnp.zeros_like(r.turn)
    r.turn[0:8] = small[...]
    r.small_cols[...] = jnp.transpose(r.turn[...])[0:8]
    square = (STRETCH, STRETCH)
    below = (iota(square, 1) <= iota(square, 0)).astype(f32)
    for k in range(length // STRETCH):
        rows = slice(k * STRETCH, (k + 1) * STRETCH)
        r.turn[0:heads] = r.step[:, rows].astype(f32)
        z = jnp.transpose(r.turn[...]) + small[0:1]
        dt = jnp.maximum(z, 0.0) + jnp.log1p(jnp.exp(-jnp.abs(z)))
        r.dt[rows] = dt
        ld = mm_exact(below, dt * small[1:2])
        r.ld[rows] = ld
        r.ldt[k] = jnp.transpose(ld)[0:8]


def widen(columns, pair):
    first, second = columns[:, 2 * pair : 2 * pair + 1], columns[:, 2 * pair + 1 : 2 * pair + 2]
    low = iota((1, LANES), 1) < HEAD_DIM
    return jnp.where(low, first, second)


def widen_all(row, pairs):
    return jnp.concatenate([widen(row, p) for p in range(pairs)], axis=1)


def split_pair(x):
    low = iota(x.shape, 1) < HEAD_DIM
    zero = jnp.zeros_like(x)
    return jnp.concatenate([jnp.where(low, x, zero), jnp.where(low, zero, x)], axis=0)


def decay_of(ld, ldt, head):
    square = (STRETCH, STRETCH)
    causal = iota(square, 1) <= iota(square, 0)
    spread = ld[:, head : head + 1] - ldt[head : head + 1]
    return jnp.exp(jnp.where(causal, spread, -1e30))


def ssm_forward(r):
    length, channels = r.branch.shape
    pairs = channels // LANES
    prepare(r)
    small = r.small
    r.state[...] = jnp.zeros_like(r.state)

    @pl.loop(0, length // STRETCH)
    def _(k):
        rows = pl.ds(pl.multiple_of(k * STRETCH, STRETCH), STRETCH)
        i_wide, r_wide = r.i[rows], r.r[rows]
        i_now, r_now = i_wide.astype(bf16), r_wide.astype(bf16)
        ld, ldt, dt = r.ld[rows], r.ldt[k], r.dt[rows]
        scores = mm_exact(r_wide, i_wide, NT)
        enter = jnp.exp(ld)
        last = ld[STRETCH - 1 : STRETCH]
        leave = jnp.exp(last - ld)
        held = r.state[...].astype(bf16)
        r.sprev[k] = held
        across = mm(r_now, held)
        carried = []
        squares = jnp.zeros((STRETCH, LANES), f32)
        for p in range(pairs):
            cols = slice(p * LANES, (p + 1) * LANES)
            value = r.v[rows, cols]
            stepped = widen(dt, p) * value
            weights = jnp.concatenate(
                [(scores * decay_of(ld, ldt, 2 * p + h)).astype(bf16) for h in range(2)], axis=1
            )
            y = mm(weights, split_pair(stepped.astype(bf16)))
            y = y + widen(enter, p) * across[:, cols]
            y = y + widen(small[2:3], p) * value
            r.y[rows, cols] = y
            gate = r.gate[rows, cols].astype(f32)
            gated = y * (gate * sigmoid(gate))
            squares = squares + gated * gated
            carried.append((widen(leave, p) * stepped).astype(bf16))
        squares = jnp.sum(squares, axis=1, keepdims=True)
        r.squares[rows] = jnp.broadcast_to(squares, (STRETCH, LANES))
        fresh = mm(i_now, jnp.concatenate(carried, axis=1), TN)
        r.state[...] = widen_all(jnp.exp(last), pairs) * r.state[...] + fresh


def ssm_backward(r):
    length, channels = r.branch.shape
    pairs = channels // LANES
    small = r.small
    r.state[...] = jnp.zeros_like(r.state)
    square = (STRETCH, STRETCH)
    row, col = iota(square, 0), iota(square, 1)
    before = (row < col).astype(bf16)
    before32 = (row < col).astype(f32)
    since32 = (row >= col).astype(f32)
    own = (iota((8, channels), 1) // HEAD_DIM == iota((8, channels), 0)).astype(bf16)

    @pl.loop(0, length // STRETCH)
    def _(turn):
        k = length // STRETCH - 1 - turn
        rows = pl.ds(pl.multiple_of(k * STRETCH, STRETCH), STRETCH)
        i_wide, r_wide = r.i[rows], r.r[rows]
        i_now, r_now = i_wide.astype(bf16), r_wide.astype(bf16)
        ld, ldt, dt = r.ld[rows], r.ldt[k], r.dt[rows]
        scores = mm_exact(r_wide, i_wide, NT)
        enter = jnp.exp(ld)
        last = ld[STRETCH - 1 : STRETCH]
        leave = jnp.exp(last - ld)
        held = r.sprev[k]
        across = mm(r_now, held)
        entering, leaving, crossed, direct, left = [], [], [], [], []
        grad_after = r.state[...].astype(bf16)
        from_state = mm(i_now, grad_after)
        grad_scores = jnp.zeros(square, f32)
        straddle = []
        for p in range(pairs):
            cols = slice(p * LANES, (p + 1) * LANES)
            value = r.v[rows, cols]
            dt_wide = widen(dt, p)
            stepped = dt_wide * value
            gate = r.gate[rows, cols].astype(f32)
            gg = r.gg[rows, cols]
            r.grad_gate[rows, cols] = (gg * r.y[rows, cols] * silu_slope(gate)).astype(bf16)
            gy = gg * (gate * sigmoid(gate))
            gys = split_pair(gy.astype(bf16))
            grad_weights = mm(gys, stepped.astype(bf16), NT)
            weights = []
            for h in range(2):
                decay = decay_of(ld, ldt, 2 * p + h)
                weight = scores * decay
                weights.append(weight.astype(bf16))
                grad_weight = grad_weights[h * STRETCH : (h + 1) * STRETCH]
                grad_scores = grad_scores + grad_weight * decay
                crossing = mm((grad_weight * weight).astype(bf16), before)
                straddle.append(
                    jnp.sum(jnp.where(row >= col, crossing, 0.0), axis=0, keepdims=True)
                )
            grad_stepped = mm(jnp.concatenate(weights, axis=0), gys, TN)
            wide_enter = widen(enter, p) * gy
            entering.append(wide_enter.astype(bf16))
            crossed.append((wide_enter * across[:, cols]).astype(bf16))
            wide_leave = widen(leave, p)
            back = wide_leave * from_state[:, cols]
            grad_stepped = grad_stepped + back
            left.append((back * stepped).astype(bf16))
            leaving.append((wide_leave * stepped).astype(bf16))
            direct.append((grad_stepped * value).astype(bf16))
            r.gv[rows, cols] = dt_wide * grad_stepped + widen(small[2:3], p) * gy
        entering = jnp.concatenate(entering, axis=1)
        gs = grad_scores.astype(bf16)
        r.gr[rows] = mm(gs, i_now) + mm(entering, held, NT)
        grad_in = mm(gs, r_now, TN)
        grad_in = grad_in + mm(jnp.concatenate(leaving, axis=1), grad_after, NT)
        r.gi[rows] = grad_in
        to_heads = lambda parts: mm(own, jnp.concatenate(parts, axis=1), NT)
        grad_x = jnp.concatenate(straddle, axis=0)
        grad_x = grad_x + mm_exact(to_heads(crossed), since32)
        grad_x = grad_x + mm_exact(to_heads(left), before32)
        faded = widen_all(jnp.exp(last), pairs) * r.state[...]
        kept = jnp.sum(faded * held.astype(f32), axis=0, keepdims=True)
        grad_x = grad_x + jnp.sum(own.astype(f32) * kept, axis=1, keepdims=True)
        grad_dt = to_heads(direct) + grad_x * r.small_cols[:, 1:2]
        z = r.step[:, rows].astype(f32) + r.small_cols[:, 0:1]
        r.grad_step[:, rows] = (grad_dt * sigmoid(z)).astype(bf16)
        r.state[...] = faded + mm(r_now, entering, TN)

    for cols in panels(channels):
        taps = r.conv_inner[:, cols].astype(f32)
        pre = conv(r.branch[:, cols].astype(f32), taps)
        r.grad_branch[:, cols] = conv_back(r.gv[:, cols] * silu_slope(pre), taps).astype(bf16)
    for source, first, grad in ((r.inp, 0, r.gi), (r.ro, GROUPS, r.gr)):
        for cols in panels(STATE):
            taps = group_taps(r, first, cols)
            pre = conv(source[:, cols].astype(f32), taps)
            grad[:, cols] = conv_back(grad[:, cols] * silu_slope(pre), taps)


def at_rows(start, count):
    return pl.ds(pl.multiple_of(start, count), count)


class Links:
    def __init__(self, send, receive):
        self.send, self.receive, self.count = send, receive, 0

    def start(self, source, target, device):
        slot = self.count
        self.count += 1
        copy = pltpu.make_async_remote_copy(
            src_ref=source,
            dst_ref=target,
            send_sem=self.send.at[slot],
            recv_sem=self.receive.at[slot],
            device_id=device,
            device_id_type=pl.DeviceIdType.MESH,
        )
        copy.start()
        return copy


class Gather:
    def __init__(self, links, block, pair, ring, devices, own=None, core=None):
        self.links, self.block, self.pair, self.ring = links, block, pair, ring
        self.to_pair, self.up, self.down = devices
        self.core = core
        self.own = block(pair, ring, None) if own is None else own
        self.sent, self.relays = [], []

    def place(self, other, step, half=None):
        pair = lax.rem(self.pair + other, 2)
        return self.block(pair, lax.rem(self.ring + step + 4, 4), half)

    def go(self, source, target, device):
        self.sent.append(self.links.start(source, target, device))

    def relay(self, source, target):
        if self.core is not None:
            self.relays.append(self.links.start(source, target, self.core))

    def begin(self):
        here = self.place(0, 0)
        for device in (self.to_pair, self.up, self.down):
            self.go(self.own, here, device)
        self.relay(self.own, here)

    def pass_on(self, number):
        self.sent[number].wait_recv()
        if number == 0:
            piece = self.place(1, 0)
            self.go(piece, piece, self.up)
            self.go(piece, piece, self.down)
        elif number <= 4:
            other, upward = (number - 1) // 2, number % 2 == 1
            step, half = (-1, 0) if upward else (1, 1)
            piece = self.place(other, step)
            part = self.place(other, step, half)
            self.go(part, part, self.up if upward else self.down)
        else:
            other, upward = (number - 5) // 2, number % 2 == 1
            piece = self.place(other, 2, 0 if upward else 1)
        self.relay(piece, piece)

    def finish(self):
        for copy in self.relays:
            copy.wait_recv()

    def close(self):
        for copy in self.sent + self.relays:
            copy.wait_send()


COPIES = 96
LOCALS = 6


def work_scratch(length, channels, width, spread, count):
    own_rows, part = length // count, width // spread
    halfway = width // 2
    return dict(
        v=pltpu.VMEM((length, channels), f32),
        i=pltpu.VMEM((length, STATE), f32),
        r=pltpu.VMEM((length, STATE), f32),
        dt=pltpu.VMEM((length, LANES), f32),
        ld=pltpu.VMEM((length, LANES), f32),
        ldt=pltpu.VMEM((length // STRETCH, 8, LANES), f32),
        small=pltpu.VMEM((8, LANES), f32),
        state=pltpu.VMEM((STATE, channels), f32),
        sprev=pltpu.VMEM((length // STRETCH, STATE, channels), bf16),
        y=pltpu.VMEM((length, channels), f32),
        squares=pltpu.VMEM((length, LANES), f32),
        squares_there=pltpu.VMEM((length, LANES), f32),
        inv=pltpu.VMEM((length, LANES), f32),
        within=pltpu.VMEM((length, LANES), f32),
        within_there=pltpu.VMEM((length, LANES), f32),
        gv=pltpu.VMEM((length, channels), f32),
        gg=pltpu.VMEM((length, channels), f32),
        gi=pltpu.VMEM((length, STATE), f32),
        gr=pltpu.VMEM((length, STATE), f32),
        g_there=pltpu.VMEM((length, STATE), f32),
        g_sum=pltpu.VMEM((length, STATE), bf16),
        turn=pltpu.VMEM((LANES, LANES), f32),
        small_cols=pltpu.VMEM((8, LANES), f32),
        inp=pltpu.VMEM((length, STATE), bf16),
        ro=pltpu.VMEM((length, STATE), bf16),
        w=pltpu.VMEM((channels, width), bf16),
        w_there=pltpu.VMEM((channels, halfway), bf16),
        normed=pltpu.VMEM((length, channels), bf16),
        normed_there=pltpu.VMEM((length, channels), bf16),
        normed_all=pltpu.VMEM((spread, channels, length), bf16),
        cot_part=pltpu.VMEM((spread, length, part), bf16),
        cot_full=pltpu.VMEM((length, width), bf16),
        product=pltpu.VMEM((channels, part), f32),
        block=pltpu.VMEM((channels, part), bf16),
        layer_part=pltpu.VMEM((length, halfway), bf16),
        layer_there=pltpu.VMEM((count, own_rows, halfway), bf16),
        sends=pltpu.SemaphoreType.DMA((COPIES,)),
        receives=pltpu.SemaphoreType.DMA((COPIES,)),
        local_sems=pltpu.SemaphoreType.DMA((LOCALS,)),
    )


def mixer(names, spread, count, *refs):
    r = SimpleNamespace(**dict(zip(names, refs)))
    length, channels = r.branch.shape
    width = r.matrix.shape[1]
    part, halfway, own_rows = width // spread, width // 2, length // count
    group_span = HEADS * HEAD_DIM // GROUPS
    dp, place = lax.axis_index("dp"), lax.axis_index("tensor")
    core = lax.rem(place, 2)
    other_core = {"tensor": place + 1 - 2 * core}
    r.group = place // 2

    barrier = pltpu.get_barrier_semaphore()
    for k in range(1, spread):
        device = {"dp": lax.rem(dp + k, spread)}
        pl.semaphore_signal(barrier, inc=1, device_id=device, device_id_type=pl.DeviceIdType.MESH)
    for k in range(1, count):
        device = {"tensor": lax.rem(place + k, count)}
        pl.semaphore_signal(barrier, inc=1, device_id=device, device_id_type=pl.DeviceIdType.MESH)

    def bring(source, target, slot):
        copy = pltpu.make_async_copy(source, target, r.local_sems.at[slot])
        copy.start()
        return copy

    input_columns = pl.ds(pl.multiple_of(r.group * STATE, STATE), STATE)
    readout_columns = pl.ds(pl.multiple_of((GROUPS + r.group) * STATE, STATE), STATE)
    bring_in = bring(r.group_proj.at[:, input_columns], r.inp, 0)
    bring_ro = bring(r.group_proj.at[:, readout_columns], r.ro, 1)
    own_part = pl.ds(pl.multiple_of(dp * part, part), part)
    bring_part = bring(
        r.cotangent.at[:, own_part], r.cot_part.at[dp, at_rows(place * own_rows, own_rows)], 2
    )
    bring_full = bring(r.cotangent, r.cot_full.at[at_rows(place * own_rows, own_rows)], 3)
    bring_w = bring(r.matrix, r.w, 4)
    pl.semaphore_wait(barrier, spread + count - 2)

    links = Links(r.sends, r.receives)
    parts_sent = []
    for k in range(1, spread):
        to = lax.rem(dp + k, spread)
        source = r.cotangent.at[:, pl.ds(pl.multiple_of(to * part, part), part)]
        target = r.cot_part.at[dp, at_rows(place * own_rows, own_rows)]
        parts_sent.append(links.start(source, target, {"dp": to}))
    their_half = pl.ds(pl.multiple_of((1 - core) * halfway, halfway), halfway)
    w_sent = links.start(r.matrix.at[:, their_half], r.w_there, other_core)

    bring_in.wait()
    bring_ro.wait()
    ssm_forward(r)
    squares_sent = links.start(r.squares, r.squares_there, other_core)

    chip = place // 2
    column, level = chip // 4, lax.rem(chip, 4)

    def tensor_id(pair, ring):
        return (pair * 4 + ring) * 2 + core

    tensor_devices = [
        {"tensor": tensor_id(1 - column, level)},
        {"tensor": tensor_id(column, lax.rem(level + 1, 4))},
        {"tensor": tensor_id(column, lax.rem(level + 3, 4))},
    ]
    side, depth = dp // 4, lax.rem(dp, 4)
    dp_devices = [
        {"dp": (1 - side) * 4 + depth},
        {"dp": side * 4 + lax.rem(depth + 1, 4)},
        {"dp": side * 4 + lax.rem(depth + 3, 4)},
    ]

    def part_block(pair, ring, half):
        rows = at_rows(tensor_id(pair, ring) * own_rows, own_rows)
        if half is None:
            return r.cot_part.at[:, rows]
        return r.cot_part.at[half * (spread // 2) : (half + 1) * (spread // 2), rows]

    def full_block(pair, ring, half):
        rows = at_rows(tensor_id(pair, ring) * own_rows, own_rows)
        if half is None:
            return r.cot_full.at[rows]
        return r.cot_full.at[rows, half * halfway : (half + 1) * halfway]

    def normed_block(pair, ring, half):
        if half is None:
            return r.normed_all.at[pair * 4 + ring]
        rows = slice(half * (channels // 2), (half + 1) * (channels // 2))
        return r.normed_all.at[pair * 4 + ring, rows]

    def matrix_block(pair, ring, half):
        cols = pl.ds(pl.multiple_of((pair * 4 + ring) * part, part), part)
        if half is None:
            return r.grad_matrix.at[:, cols]
        rows = slice(half * (channels // 2), (half + 1) * (channels // 2))
        return r.grad_matrix.at[rows, cols]

    gather_part = Gather(links, part_block, column, level, tensor_devices, core=other_core)
    gather_full = Gather(
        links, full_block, column, level, tensor_devices, own=r.cotangent, core=other_core
    )
    gather_normed = Gather(links, normed_block, side, depth, dp_devices)
    gather_matrix = Gather(links, matrix_block, side, depth, dp_devices, own=r.block)

    bring_part.wait()
    for copy in parts_sent:
        copy.wait_recv()
    gather_part.begin()

    squares_sent.wait_recv()
    r.inv[...] = lax.rsqrt((r.squares[...] + r.squares_there[...]) / group_span + epsilon)
    for cols in panels(channels):
        gate = r.gate[:, cols].astype(f32)
        gated = r.y[:, cols] * (gate * sigmoid(gate))
        normed = gated * r.inv[...] * r.gain[:, cols]
        r.normed[:, cols] = normed.astype(bf16)
        r.normed_all[dp, cols] = jnp.transpose(normed).astype(bf16)
    gather_normed.begin()
    normed_sent = links.start(r.normed, r.normed_there, other_core)

    gather_part.pass_on(0)
    w_sent.wait_recv()
    bring_w.wait()
    normed_sent.wait_recv()
    tile = 256

    @pl.loop(0, halfway // tile)
    def _(step):
        cols = pl.ds(pl.multiple_of(step * tile, tile), tile)
        wide = pl.ds(pl.multiple_of(core * halfway + step * tile, tile), tile)
        total = mm(r.normed[...], r.w[:, wide])
        total = total + mm(r.normed_there[...], r.w_there[:, cols])
        r.layer_part[:, cols] = total.astype(bf16)

    gather_part.pass_on(1)
    gather_part.pass_on(2)
    for number in range(3):
        gather_normed.pass_on(number)
    gather_part.pass_on(3)
    gather_part.pass_on(4)
    gather_normed.pass_on(3)
    gather_normed.pass_on(4)
    gather_full.begin()
    for number in range(5, 9):
        gather_part.pass_on(number)
    gather_part.finish()

    def add_product(index, first=False):
        @pl.loop(0, part // tile)
        def _(step):
            cols = pl.ds(pl.multiple_of(step * tile, tile), tile)
            term = mm(r.normed_all[index], r.cot_part[index, :, cols])
            if first:
                r.product[:, cols] = term
            else:
                r.product[:, cols] += term

    add_product(dp, first=True)
    add_product((1 - side) * 4 + depth)
    for step in (1, 3):
        add_product(side * 4 + lax.rem(depth + step, 4))
        add_product((1 - side) * 4 + lax.rem(depth + step, 4))
    for number in range(5, 9):
        gather_normed.pass_on(number)
    add_product(side * 4 + lax.rem(depth + 2, 4))
    add_product((1 - side) * 4 + lax.rem(depth + 2, 4))
    r.block[...] = r.product[...].astype(bf16)
    gather_matrix.begin()
    bring_block = bring(r.block, matrix_block(side, depth, None), 5)

    for number in range(5):
        gather_full.pass_on(number)
    layers_sent = []
    for k in range(1, count):
        to = lax.rem(place + k, count)
        source = r.layer_part.at[at_rows(to * own_rows, own_rows)]
        layers_sent.append(links.start(source, r.layer_there.at[place], {"tensor": to}))
    for number in range(3):
        gather_matrix.pass_on(number)
    for number in range(5, 9):
        gather_full.pass_on(number)
    bring_full.wait()
    gather_full.finish()

    r.gg[...] = jnp.zeros_like(r.gg)
    deep = 512

    @pl.loop(0, width // deep)
    def _(step):
        cols = pl.ds(pl.multiple_of(step * deep, deep), deep)
        r.gg[...] += mm(r.cot_full[:, cols], r.w[:, cols], NT)

    within = jnp.zeros((length, LANES), f32)
    for cols in panels(channels):
        gate = r.gate[:, cols].astype(f32)
        gated = r.y[:, cols] * (gate * sigmoid(gate))
        scaled = r.gain[:, cols] * r.gg[:, cols]
        r.gg[:, cols] = scaled
        within = within + gated * scaled
    within = jnp.sum(within, axis=1, keepdims=True)
    r.within[...] = jnp.broadcast_to(within, (length, LANES))
    within_sent = links.start(r.within, r.within_there, other_core)
    gather_matrix.pass_on(3)
    gather_matrix.pass_on(4)
    within_sent.wait_recv()
    inv = r.inv[...]
    shared = inv * inv * inv * (r.within[...] + r.within_there[...]) * (1.0 / group_span)
    for cols in panels(channels):
        gate = r.gate[:, cols].astype(f32)
        gated = r.y[:, cols] * (gate * sigmoid(gate))
        r.gg[:, cols] = inv * r.gg[:, cols] - gated * shared
    ssm_backward(r)

    given = links.count
    links.count += 1

    def give(source):
        return pltpu.make_async_remote_copy(
            src_ref=source,
            dst_ref=r.g_there,
            send_sem=links.send.at[given],
            recv_sem=links.receive.at[given],
            device_id=other_core,
            device_id_type=pl.DeviceIdType.MESH,
        )

    @pl.when(core == 0)
    def _():
        give(r.gr).start()

    @pl.when(core == 1)
    def _():
        give(r.gi).start()

    for number in range(5, 9):
        gather_matrix.pass_on(number)
    r.layer_there[place] = r.layer_part[at_rows(place * own_rows, own_rows)]
    for copy in layers_sent:
        copy.wait_recv()
    for half in range(2):
        total = r.layer_there[half].astype(f32)
        for source in range(half + 2, count, 2):
            total = total + r.layer_there[source].astype(f32)
        r.layer_out[:, half * halfway : (half + 1) * halfway] = total.astype(bf16)

    give(r.gr).wait()

    @pl.when(core == 0)
    def _():
        r.g_sum[...] = (r.gi[...] + r.g_there[...]).astype(bf16)

    @pl.when(core == 1)
    def _():
        r.g_sum[...] = (r.gr[...] + r.g_there[...]).astype(bf16)

    owner = chip + core * (count // 2)

    @pl.when(owner == place)
    def _():
        r.grad_groups[...] = r.g_sum[...]

    @pl.when(owner != place)
    def _():
        links.start(r.g_sum, r.grad_groups, {"tensor": owner}).wait()

    bring_block.wait()
    for copy in parts_sent + layers_sent + [w_sent, squares_sent, normed_sent, within_sent]:
        copy.wait_send()
    for gather in (gather_part, gather_full, gather_normed, gather_matrix):
        gather.close()


def shape(dims, dtype):
    return jax.ShapeDtypeStruct(dims, dtype)


def hand_over(arrays):
    number = len(arrays)

    def body(*refs):
        sems = refs[2 * number]
        copies = [
            pltpu.make_async_copy(refs[k], refs[number + k], sems.at[k]) for k in range(number)
        ]
        for copy in copies:
            copy.start()
        for copy in copies:
            copy.wait()

    return pl.pallas_call(
        body,
        out_shape=[shape(array.shape, array.dtype) for array in arrays],
        in_specs=[pl.BlockSpec(memory_space=pltpu.HBM)] * number,
        out_specs=[pl.BlockSpec(memory_space=pltpu.HBM)] * number,
        scratch_shapes=[pltpu.SemaphoreType.DMA((number,))],
    )(*arrays)


def local(
    spread,
    count,
    branch_in,
    gate_in,
    group_proj,
    step_raw,
    conv_inner,
    conv_groups,
    step_bias,
    decay_log,
    skip_gain,
    norm_gain,
    exit_mapping_matrix,
    cotangent,
):
    length, channels = branch_in.shape
    heads = step_raw.shape[1]
    width = exit_mapping_matrix.shape[1]
    operands = dict(
        branch=branch_in,
        gate=gate_in,
        step=step_raw.T,
        conv_inner=conv_inner,
        conv_groups=conv_groups,
        step_bias=step_bias[None],
        decay_log=decay_log[None],
        skip=skip_gain[None],
        gain=norm_gain[None],
        group_proj=group_proj,
        matrix=exit_mapping_matrix,
        cotangent=cotangent,
    )
    results = dict(
        layer_out=shape((length // count, width), bf16),
        grad_branch=shape((length, channels), bf16),
        grad_gate=shape((length, channels), bf16),
        grad_groups=shape((length, STATE), bf16),
        grad_step=shape((heads, length), bf16),
        grad_matrix=shape((channels, width), bf16),
    )
    scratch = work_scratch(length, channels, width, spread, count)
    far = ("group_proj", "matrix", "cotangent", "grad_matrix")

    def spec(name):
        return pl.BlockSpec(memory_space=pl.ANY if name in far else pltpu.VMEM)

    names = list(operands) + list(results) + list(scratch)
    made = pl.pallas_call(
        functools.partial(mixer, names, spread, count),
        out_shape=list(results.values()),
        in_specs=[spec(name) for name in operands],
        out_specs=[spec(name) for name in results],
        scratch_shapes=list(scratch.values()),
        compiler_params=pltpu.CompilerParams(
            collective_id=0, has_side_effects=True, vmem_limit_bytes=62 * 2**20
        ),
    )(*operands.values())
    made = hand_over(made)
    turned = ("grad_step",)
    return tuple(array.T if name in turned else array for name, array in zip(results, made))


def solution(mesh):
    placed = (
        P("dp", "tensor"),
        P("dp", "tensor"),
        P("dp", None),
        P("dp", "tensor"),
        P(None, "tensor"),
        P(),
        P("tensor"),
        P("tensor"),
        P("tensor"),
        P("tensor"),
        P("tensor", None),
        P(("dp", "tensor"), None),
    )
    return jax.shard_map(
        functools.partial(local, mesh.shape["dp"], mesh.shape["tensor"]),
        mesh=mesh,
        in_specs=placed,
        out_specs=(
            P(("dp", "tensor"), None),
            P("dp", "tensor"),
            P("dp", "tensor"),
            P("dp", "tensor"),
            P("dp", "tensor"),
            P("tensor", None),
        ),
        check_vma=False,
    )
```

```python
import functools
from types import SimpleNamespace

import jax
import jax.numpy as jnp
from jax import lax
from jax.experimental import pallas as pl
from jax.experimental.pallas import tpu as pltpu
from jax.sharding import PartitionSpec as P

HEADS = 128
HEAD_DIM = 64
STATE = 256
GROUPS = 8
KERNEL = 4
STRETCH = 128
LANES = 128
f32, bf16 = jnp.float32, jnp.bfloat16
epsilon = 1e-05
NN = (((1,), (0,)), ((), ()))
NT = (((1,), (1,)), ((), ()))
TN = (((0,), (0,)), ((), ()))


def mm(a, b, dims=NN):
    return lax.dot_general(a, b, dims, preferred_element_type=f32)


def mm_exact(a, b, dims=NN):
    return lax.dot_general(a, b, dims, precision=lax.Precision.HIGHEST, preferred_element_type=f32)


def iota(shape, axis):
    return lax.broadcasted_iota(jnp.int32, shape, axis)


def sigmoid(x):
    return 1.0 / (1.0 + jnp.exp(-x))


def later(x, steps):
    return jnp.where(iota(x.shape, 0) >= steps, pltpu.roll(x, steps, 0), 0.0)


def earlier(x, steps):
    length = x.shape[0]
    return jnp.where(iota(x.shape, 0) < length - steps, pltpu.roll(x, length - steps, 0), 0.0)


def conv(x, taps):
    total = taps[KERNEL - 1 : KERNEL] * x
    for steps in range(1, KERNEL):
        total = total + taps[KERNEL - 1 - steps : KERNEL - steps] * later(x, steps)
    return total


def conv_back(g, taps):
    total = taps[KERNEL - 1 : KERNEL] * g
    for steps in range(1, KERNEL):
        total = total + taps[KERNEL - 1 - steps : KERNEL - steps] * earlier(g, steps)
    return total


def silu_slope(x):
    s = sigmoid(x)
    return s * (1.0 + x * (1.0 - s))


def panels(width):
    return [slice(c, c + LANES) for c in range(0, width, LANES)]


def group_taps(r, first, cols):
    start = (first + r.group) * STATE + cols.start
    return r.conv_groups[:, pl.ds(pl.multiple_of(start, LANES), LANES)].astype(f32)


def prepare(r):
    length, channels = r.branch.shape
    heads = r.step.shape[0]
    for cols in panels(channels):
        pre = conv(r.branch[:, cols].astype(f32), r.conv_inner[:, cols].astype(f32))
        r.v[:, cols] = pre * sigmoid(pre)
    for source, first, to in ((r.inp, 0, r.i), (r.ro, GROUPS, r.r)):
        for cols in panels(STATE):
            pre = conv(source[:, cols].astype(f32), group_taps(r, first, cols))
            to[:, cols] = pre * sigmoid(pre)
    small = r.small
    small[...] = jnp.zeros_like(small)
    small[0:1, 0:heads] = r.step_bias[...]
    small[1:2, 0:heads] = -jnp.exp(r.decay_log[...])
    small[2:3, 0:heads] = r.skip[...]
    r.turn[...] = jnp.zeros_like(r.turn)
    r.turn[0:8] = small[...]
    r.small_cols[...] = jnp.transpose(r.turn[...])[0:8]
    square = (STRETCH, STRETCH)
    below = (iota(square, 1) <= iota(square, 0)).astype(f32)
    for k in range(length // STRETCH):
        rows = slice(k * STRETCH, (k + 1) * STRETCH)
        r.turn[0:heads] = r.step[:, rows].astype(f32)
        z = jnp.transpose(r.turn[...]) + small[0:1]
        dt = jnp.maximum(z, 0.0) + jnp.log1p(jnp.exp(-jnp.abs(z)))
        r.dt[rows] = dt
        ld = mm_exact(below, dt * small[1:2])
        r.ld[rows] = ld
        r.ldt[k] = jnp.transpose(ld)[0:8]


def widen(columns, pair):
    first, second = columns[:, 2 * pair : 2 * pair + 1], columns[:, 2 * pair + 1 : 2 * pair + 2]
    low = iota((1, LANES), 1) < HEAD_DIM
    return jnp.where(low, first, second)


def widen_all(row, pairs):
    return jnp.concatenate([widen(row, p) for p in range(pairs)], axis=1)


def split_pair(x):
    low = iota(x.shape, 1) < HEAD_DIM
    zero = jnp.zeros_like(x)
    return jnp.concatenate([jnp.where(low, x, zero), jnp.where(low, zero, x)], axis=0)


def decay_of(ld, ldt, head):
    square = (STRETCH, STRETCH)
    causal = iota(square, 1) <= iota(square, 0)
    spread = ld[:, head : head + 1] - ldt[head : head + 1]
    return jnp.exp(jnp.where(causal, spread, -1e30))


def ssm_forward(r):
    length, channels = r.branch.shape
    pairs = channels // LANES
    prepare(r)
    small = r.small
    r.state[...] = jnp.zeros_like(r.state)

    @pl.loop(0, length // STRETCH)
    def _(k):
        rows = pl.ds(pl.multiple_of(k * STRETCH, STRETCH), STRETCH)
        i_wide, r_wide = r.i[rows], r.r[rows]
        i_now, r_now = i_wide.astype(bf16), r_wide.astype(bf16)
        ld, ldt, dt = r.ld[rows], r.ldt[k], r.dt[rows]
        scores = mm_exact(r_wide, i_wide, NT)
        enter = jnp.exp(ld)
        last = ld[STRETCH - 1 : STRETCH]
        leave = jnp.exp(last - ld)
        held = r.state[...].astype(bf16)
        r.sprev[k] = held
        across = mm(r_now, held)
        carried = []
        squares = jnp.zeros((STRETCH, LANES), f32)
        for p in range(pairs):
            cols = slice(p * LANES, (p + 1) * LANES)
            value = r.v[rows, cols]
            stepped = widen(dt, p) * value
            weights = jnp.concatenate(
                [(scores * decay_of(ld, ldt, 2 * p + h)).astype(bf16) for h in range(2)], axis=1
            )
            y = mm(weights, split_pair(stepped.astype(bf16)))
            y = y + widen(enter, p) * across[:, cols]
            y = y + widen(small[2:3], p) * value
            r.y[rows, cols] = y
            gate = r.gate[rows, cols].astype(f32)
            gated = y * (gate * sigmoid(gate))
            squares = squares + gated * gated
            carried.append((widen(leave, p) * stepped).astype(bf16))
        squares = jnp.sum(squares, axis=1, keepdims=True)
        r.squares[rows] = jnp.broadcast_to(squares, (STRETCH, LANES))
        fresh = mm(i_now, jnp.concatenate(carried, axis=1), TN)
        r.state[...] = widen_all(jnp.exp(last), pairs) * r.state[...] + fresh


def ssm_backward(r):
    length, channels = r.branch.shape
    pairs = channels // LANES
    small = r.small
    r.state[...] = jnp.zeros_like(r.state)
    square = (STRETCH, STRETCH)
    row, col = iota(square, 0), iota(square, 1)
    before = (row < col).astype(bf16)
    before32 = (row < col).astype(f32)
    since32 = (row >= col).astype(f32)
    own = (iota((8, channels), 1) // HEAD_DIM == iota((8, channels), 0)).astype(bf16)

    @pl.loop(0, length // STRETCH)
    def _(turn):
        k = length // STRETCH - 1 - turn
        rows = pl.ds(pl.multiple_of(k * STRETCH, STRETCH), STRETCH)
        i_wide, r_wide = r.i[rows], r.r[rows]
        i_now, r_now = i_wide.astype(bf16), r_wide.astype(bf16)
        ld, ldt, dt = r.ld[rows], r.ldt[k], r.dt[rows]
        scores = mm_exact(r_wide, i_wide, NT)
        enter = jnp.exp(ld)
        last = ld[STRETCH - 1 : STRETCH]
        leave = jnp.exp(last - ld)
        held = r.sprev[k]
        across = mm(r_now, held)
        entering, leaving, crossed, direct, left = [], [], [], [], []
        grad_after = r.state[...].astype(bf16)
        from_state = mm(i_now, grad_after)
        grad_scores = jnp.zeros(square, f32)
        straddle = []
        for p in range(pairs):
            cols = slice(p * LANES, (p + 1) * LANES)
            value = r.v[rows, cols]
            dt_wide = widen(dt, p)
            stepped = dt_wide * value
            gate = r.gate[rows, cols].astype(f32)
            gg = r.gg[rows, cols]
            r.grad_gate[rows, cols] = (gg * r.y[rows, cols] * silu_slope(gate)).astype(bf16)
            gy = gg * (gate * sigmoid(gate))
            gys = split_pair(gy.astype(bf16))
            grad_weights = mm(gys, stepped.astype(bf16), NT)
            weights = []
            for h in range(2):
                decay = decay_of(ld, ldt, 2 * p + h)
                weight = scores * decay
                weights.append(weight.astype(bf16))
                grad_weight = grad_weights[h * STRETCH : (h + 1) * STRETCH]
                grad_scores = grad_scores + grad_weight * decay
                crossing = mm((grad_weight * weight).astype(bf16), before)
                straddle.append(
                    jnp.sum(jnp.where(row >= col, crossing, 0.0), axis=0, keepdims=True)
                )
            grad_stepped = mm(jnp.concatenate(weights, axis=0), gys, TN)
            wide_enter = widen(enter, p) * gy
            entering.append(wide_enter.astype(bf16))
            crossed.append((wide_enter * across[:, cols]).astype(bf16))
            wide_leave = widen(leave, p)
            back = wide_leave * from_state[:, cols]
            grad_stepped = grad_stepped + back
            left.append((back * stepped).astype(bf16))
            leaving.append((wide_leave * stepped).astype(bf16))
            direct.append((grad_stepped * value).astype(bf16))
            r.gv[rows, cols] = dt_wide * grad_stepped + widen(small[2:3], p) * gy
        entering = jnp.concatenate(entering, axis=1)
        gs = grad_scores.astype(bf16)
        r.gr[rows] = mm(gs, i_now) + mm(entering, held, NT)
        grad_in = mm(gs, r_now, TN)
        grad_in = grad_in + mm(jnp.concatenate(leaving, axis=1), grad_after, NT)
        r.gi[rows] = grad_in
        to_heads = lambda parts: mm(own, jnp.concatenate(parts, axis=1), NT)
        grad_x = jnp.concatenate(straddle, axis=0)
        grad_x = grad_x + mm_exact(to_heads(crossed), since32)
        grad_x = grad_x + mm_exact(to_heads(left), before32)
        faded = widen_all(jnp.exp(last), pairs) * r.state[...]
        kept = jnp.sum(faded * held.astype(f32), axis=0, keepdims=True)
        grad_x = grad_x + jnp.sum(own.astype(f32) * kept, axis=1, keepdims=True)
        grad_dt = to_heads(direct) + grad_x * r.small_cols[:, 1:2]
        z = r.step[:, rows].astype(f32) + r.small_cols[:, 0:1]
        r.grad_step[:, rows] = (grad_dt * sigmoid(z)).astype(bf16)
        r.state[...] = faded + mm(r_now, entering, TN)

    for cols in panels(channels):
        taps = r.conv_inner[:, cols].astype(f32)
        pre = conv(r.branch[:, cols].astype(f32), taps)
        r.grad_branch[:, cols] = conv_back(r.gv[:, cols] * silu_slope(pre), taps).astype(bf16)
    for source, first, grad in ((r.inp, 0, r.gi), (r.ro, GROUPS, r.gr)):
        for cols in panels(STATE):
            taps = group_taps(r, first, cols)
            pre = conv(source[:, cols].astype(f32), taps)
            grad[:, cols] = conv_back(grad[:, cols] * silu_slope(pre), taps)


def at_rows(start, count):
    return pl.ds(pl.multiple_of(start, count), count)


class Links:
    def __init__(self, send, receive):
        self.send, self.receive, self.count = send, receive, 0

    def start(self, source, target, device):
        slot = self.count
        self.count += 1
        copy = pltpu.make_async_remote_copy(
            src_ref=source,
            dst_ref=target,
            send_sem=self.send.at[slot],
            recv_sem=self.receive.at[slot],
            device_id=device,
            device_id_type=pl.DeviceIdType.MESH,
        )
        copy.start()
        return copy


class Gather:
    def __init__(self, links, block, pair, ring, devices, own=None, core=None, store=None):
        self.links, self.block, self.pair, self.ring = links, block, pair, ring
        self.to_pair, self.up, self.down = devices
        self.core, self.store = core, store
        self.own = block(pair, ring, None) if own is None else own
        self.sent, self.relays = [], []

    def place(self, other, step, half=None):
        pair = lax.rem(self.pair + other, 2)
        return self.block(pair, lax.rem(self.ring + step + 4, 4), half)

    def go(self, source, target, device):
        self.sent.append(self.links.start(source, target, device))

    def relay(self, source, target):
        if self.core is not None:
            self.relays.append(self.links.start(source, target, self.core))

    def begin(self):
        here = self.place(0, 0)
        for device in (self.to_pair, self.up, self.down):
            self.go(self.own, here, device)
        self.relay(self.own, here)

    def pass_on(self, number):
        self.sent[number].wait_recv()
        if number == 0:
            piece = self.place(1, 0)
            self.go(piece, piece, self.up)
            self.go(piece, piece, self.down)
        elif number <= 4:
            other, upward = (number - 1) // 2, number % 2 == 1
            step, half = (-1, 0) if upward else (1, 1)
            piece = self.place(other, step)
            part = self.place(other, step, half)
            self.go(part, part, self.up if upward else self.down)
        else:
            other, upward = (number - 5) // 2, number % 2 == 1
            piece = self.place(other, 2, 0 if upward else 1)
        self.relay(piece, piece)
        if self.store is not None:
            self.store(*self.arrived(number))

    def arrived(self, number):
        other, upward = (0, True) if number == 0 else ((number - 1) % 4 // 2, number % 2 == 1)
        if number == 0:
            return 1 - self.pair, self.ring
        step = 2 if number > 4 else (-1 if upward else 1)
        pair = lax.rem(self.pair + other, 2)
        half = None if number < 5 else (0 if upward else 1)
        return pair, lax.rem(self.ring + step + 4, 4), half

    def finish(self):
        for copy in self.relays:
            copy.wait_recv()

    def close(self):
        for copy in self.sent + self.relays:
            copy.wait_send()


COPIES = 96
LOCALS = 15


def work_scratch(length, channels, width, spread, count):
    own_rows, part = length // count, width // spread
    halfway = width // 2
    return dict(
        v=pltpu.VMEM((length, channels), f32),
        i=pltpu.VMEM((length, STATE), f32),
        r=pltpu.VMEM((length, STATE), f32),
        dt=pltpu.VMEM((length, LANES), f32),
        ld=pltpu.VMEM((length, LANES), f32),
        ldt=pltpu.VMEM((length // STRETCH, 8, LANES), f32),
        small=pltpu.VMEM((8, LANES), f32),
        state=pltpu.VMEM((STATE, channels), f32),
        sprev=pltpu.VMEM((length // STRETCH, STATE, channels), bf16),
        y=pltpu.VMEM((length, channels), f32),
        squares=pltpu.VMEM((length, LANES), f32),
        squares_there=pltpu.VMEM((length, LANES), f32),
        inv=pltpu.VMEM((length, LANES), f32),
        within=pltpu.VMEM((length, LANES), f32),
        within_there=pltpu.VMEM((length, LANES), f32),
        gv=pltpu.VMEM((length, channels), f32),
        gg=pltpu.VMEM((length, channels), f32),
        gi=pltpu.VMEM((length, STATE), f32),
        gr=pltpu.VMEM((length, STATE), f32),
        g_there=pltpu.VMEM((length, STATE), f32),
        g_sum=pltpu.VMEM((length, STATE), bf16),
        turn=pltpu.VMEM((LANES, LANES), f32),
        small_cols=pltpu.VMEM((8, LANES), f32),
        inp=pltpu.VMEM((length, STATE), bf16),
        ro=pltpu.VMEM((length, STATE), bf16),
        w=pltpu.VMEM((channels, width), bf16),
        w_there=pltpu.VMEM((channels, halfway), bf16),
        normed=pltpu.VMEM((length, channels), bf16),
        normed_there=pltpu.VMEM((length, channels), bf16),
        normed_all=pltpu.VMEM((spread, channels, length), bf16),
        cot_part=pltpu.VMEM((spread, length, part), bf16),
        cot_full=pltpu.VMEM((length, width), bf16),
        product=pltpu.VMEM((channels, part), f32),
        block=pltpu.VMEM((channels, part), bf16),
        layer_part=pltpu.VMEM((length, halfway), bf16),
        layer_there=pltpu.VMEM((count, own_rows, halfway), bf16),
        sends=pltpu.SemaphoreType.DMA((COPIES,)),
        receives=pltpu.SemaphoreType.DMA((COPIES,)),
        ready=pltpu.SemaphoreType.REGULAR,
        local_sems=pltpu.SemaphoreType.DMA((LOCALS,)),
    )


def mixer(names, spread, count, *refs):
    r = SimpleNamespace(**dict(zip(names, refs)))
    length, channels = r.branch.shape
    width = r.matrix.shape[1]
    part, halfway, own_rows = width // spread, width // 2, length // count
    group_span = HEADS * HEAD_DIM // GROUPS
    dp, place = lax.axis_index("dp"), lax.axis_index("tensor")
    core = lax.rem(place, 2)
    other_core = {"tensor": place + 1 - 2 * core}
    r.group = place // 2

    barrier = pltpu.get_barrier_semaphore()
    for k in range(1, spread):
        device = {"dp": lax.rem(dp + k, spread)}
        pl.semaphore_signal(barrier, inc=1, device_id=device, device_id_type=pl.DeviceIdType.MESH)
    for k in range(1, count):
        device = {"tensor": lax.rem(place + k, count)}
        pl.semaphore_signal(barrier, inc=1, device_id=device, device_id_type=pl.DeviceIdType.MESH)

    def bring(source, target, slot):
        copy = pltpu.make_async_copy(source, target, r.local_sems.at[slot])
        copy.start()
        return copy

    input_columns = pl.ds(pl.multiple_of(r.group * STATE, STATE), STATE)
    readout_columns = pl.ds(pl.multiple_of((GROUPS + r.group) * STATE, STATE), STATE)
    bring_in = bring(r.group_proj.at[:, input_columns], r.inp, 0)
    bring_ro = bring(r.group_proj.at[:, readout_columns], r.ro, 1)
    own_part = pl.ds(pl.multiple_of(dp * part, part), part)
    bring_part = bring(
        r.cotangent.at[:, own_part], r.cot_part.at[dp, at_rows(place * own_rows, own_rows)], 2
    )
    bring_full = bring(r.cotangent, r.cot_full.at[at_rows(place * own_rows, own_rows)], 3)
    bring_w = bring(r.matrix, r.w, 4)
    pl.semaphore_wait(barrier, spread + count - 2)

    links = Links(r.sends, r.receives)
    parts_sent = []
    for k in range(1, spread):
        to = lax.rem(dp + k, spread)
        source = r.cotangent.at[:, pl.ds(pl.multiple_of(to * part, part), part)]
        target = r.cot_part.at[dp, at_rows(place * own_rows, own_rows)]
        parts_sent.append(links.start(source, target, {"dp": to}))
    their_half = pl.ds(pl.multiple_of((1 - core) * halfway, halfway), halfway)
    w_sent = links.start(r.matrix.at[:, their_half], r.w_there, other_core)

    bring_in.wait()
    bring_ro.wait()
    ssm_forward(r)
    squares_sent = links.start(r.squares, r.squares_there, other_core)

    chip = place // 2
    column, level = chip // 4, lax.rem(chip, 4)

    def tensor_id(pair, ring):
        return (pair * 4 + ring) * 2 + core

    tensor_devices = [
        {"tensor": tensor_id(1 - column, level)},
        {"tensor": tensor_id(column, lax.rem(level + 1, 4))},
        {"tensor": tensor_id(column, lax.rem(level + 3, 4))},
    ]
    side, depth = dp // 4, lax.rem(dp, 4)
    dp_devices = [
        {"dp": (1 - side) * 4 + depth},
        {"dp": side * 4 + lax.rem(depth + 1, 4)},
        {"dp": side * 4 + lax.rem(depth + 3, 4)},
    ]

    def part_block(pair, ring, half):
        rows = at_rows(tensor_id(pair, ring) * own_rows, own_rows)
        if half is None:
            return r.cot_part.at[:, rows]
        return r.cot_part.at[half * (spread // 2) : (half + 1) * (spread // 2), rows]

    def full_block(pair, ring, half):
        rows = at_rows(tensor_id(pair, ring) * own_rows, own_rows)
        if half is None:
            return r.cot_full.at[rows]
        return r.cot_full.at[rows, half * halfway : (half + 1) * halfway]

    def normed_block(pair, ring, half):
        if half is None:
            return r.normed_all.at[pair * 4 + ring]
        rows = slice(half * (channels // 2), (half + 1) * (channels // 2))
        return r.normed_all.at[pair * 4 + ring, rows]

    def matrix_block(pair, ring, half):
        index = pair * 4 + ring
        if half is None:
            return r.cot_part.at[index]
        return r.cot_part.at[index, half * (channels // 2) : (half + 1) * (channels // 2)]

    stored = []

    def store(pair, ring, half=None):
        cols = pl.ds(pl.multiple_of((pair * 4 + ring) * part, part), part)
        target = r.grad_matrix.at[:, cols]
        if half is not None:
            target = r.grad_matrix.at[half * (channels // 2) : (half + 1) * (channels // 2), cols]
        stored.append(bring(matrix_block(pair, ring, half), target, 5 + len(stored)))

    gather_part = Gather(links, part_block, column, level, tensor_devices, core=other_core)
    gather_full = Gather(
        links, full_block, column, level, tensor_devices, own=r.cotangent, core=other_core
    )
    gather_normed = Gather(links, normed_block, side, depth, dp_devices)
    gather_matrix = Gather(
        links, matrix_block, side, depth, dp_devices, own=r.block, store=store
    )

    bring_part.wait()
    for copy in parts_sent:
        copy.wait_recv()
    gather_part.begin()

    squares_sent.wait_recv()
    r.inv[...] = lax.rsqrt((r.squares[...] + r.squares_there[...]) / group_span + epsilon)
    for cols in panels(channels):
        gate = r.gate[:, cols].astype(f32)
        gated = r.y[:, cols] * (gate * sigmoid(gate))
        normed = gated * r.inv[...] * r.gain[:, cols]
        r.normed[:, cols] = normed.astype(bf16)
        r.normed_all[dp, cols] = jnp.transpose(normed).astype(bf16)
    gather_normed.begin()
    normed_sent = links.start(r.normed, r.normed_there, other_core)

    gather_part.pass_on(0)
    w_sent.wait_recv()
    bring_w.wait()
    normed_sent.wait_recv()
    tile = 256

    @pl.loop(0, halfway // tile)
    def _(step):
        cols = pl.ds(pl.multiple_of(step * tile, tile), tile)
        wide = pl.ds(pl.multiple_of(core * halfway + step * tile, tile), tile)
        total = mm(r.normed[...], r.w[:, wide])
        total = total + mm(r.normed_there[...], r.w_there[:, cols])
        r.layer_part[:, cols] = total.astype(bf16)

    gather_part.pass_on(1)
    gather_part.pass_on(2)
    for number in range(3):
        gather_normed.pass_on(number)
    gather_part.pass_on(3)
    gather_part.pass_on(4)
    gather_normed.pass_on(3)
    gather_normed.pass_on(4)
    gather_full.begin()
    for number in range(5, 9):
        gather_part.pass_on(number)
    gather_part.finish()

    def add_product(index, first=False):
        @pl.loop(0, part // tile)
        def _(step):
            cols = pl.ds(pl.multiple_of(step * tile, tile), tile)
            term = mm(r.normed_all[index], r.cot_part[index, :, cols])
            if first:
                r.product[:, cols] = term
            else:
                r.product[:, cols] += term

    add_product(dp, first=True)
    add_product((1 - side) * 4 + depth)
    for step in (1, 3):
        add_product(side * 4 + lax.rem(depth + step, 4))
        add_product((1 - side) * 4 + lax.rem(depth + step, 4))
    for number in range(5, 9):
        gather_normed.pass_on(number)
    add_product(side * 4 + lax.rem(depth + 2, 4))
    add_product((1 - side) * 4 + lax.rem(depth + 2, 4))
    r.block[...] = r.product[...].astype(bf16)
    gather_part.close()
    for device in dp_devices:
        pl.semaphore_signal(r.ready, inc=1, device_id=device, device_id_type=pl.DeviceIdType.MESH)
    pl.semaphore_wait(r.ready, len(dp_devices))
    gather_matrix.begin()
    own_columns = pl.ds(pl.multiple_of(dp * part, part), part)
    bring_block = bring(r.block, r.grad_matrix.at[:, own_columns], 5 + 9)

    for number in range(5):
        gather_full.pass_on(number)
    layers_sent = []
    for k in range(1, count):
        to = lax.rem(place + k, count)
        source = r.layer_part.at[at_rows(to * own_rows, own_rows)]
        layers_sent.append(links.start(source, r.layer_there.at[place], {"tensor": to}))
    for number in range(3):
        gather_matrix.pass_on(number)
    for number in range(5, 9):
        gather_full.pass_on(number)
    bring_full.wait()
    gather_full.finish()

    r.gg[...] = jnp.zeros_like(r.gg)
    deep = 512

    @pl.loop(0, width // deep)
    def _(step):
        cols = pl.ds(pl.multiple_of(step * deep, deep), deep)
        r.gg[...] += mm(r.cot_full[:, cols], r.w[:, cols], NT)

    within = jnp.zeros((length, LANES), f32)
    for cols in panels(channels):
        gate = r.gate[:, cols].astype(f32)
        gated = r.y[:, cols] * (gate * sigmoid(gate))
        scaled = r.gain[:, cols] * r.gg[:, cols]
        r.gg[:, cols] = scaled
        within = within + gated * scaled
    within = jnp.sum(within, axis=1, keepdims=True)
    r.within[...] = jnp.broadcast_to(within, (length, LANES))
    within_sent = links.start(r.within, r.within_there, other_core)
    gather_matrix.pass_on(3)
    gather_matrix.pass_on(4)
    within_sent.wait_recv()
    inv = r.inv[...]
    shared = inv * inv * inv * (r.within[...] + r.within_there[...]) * (1.0 / group_span)
    for cols in panels(channels):
        gate = r.gate[:, cols].astype(f32)
        gated = r.y[:, cols] * (gate * sigmoid(gate))
        r.gg[:, cols] = inv * r.gg[:, cols] - gated * shared
    ssm_backward(r)

    given = links.count
    links.count += 1

    def give(source):
        return pltpu.make_async_remote_copy(
            src_ref=source,
            dst_ref=r.g_there,
            send_sem=links.send.at[given],
            recv_sem=links.receive.at[given],
            device_id=other_core,
            device_id_type=pl.DeviceIdType.MESH,
        )

    @pl.when(core == 0)
    def _():
        give(r.gr).start()

    @pl.when(core == 1)
    def _():
        give(r.gi).start()

    for number in range(5, 9):
        gather_matrix.pass_on(number)
    r.layer_there[place] = r.layer_part[at_rows(place * own_rows, own_rows)]
    for copy in layers_sent:
        copy.wait_recv()
    for half in range(2):
        total = r.layer_there[half].astype(f32)
        for source in range(half + 2, count, 2):
            total = total + r.layer_there[source].astype(f32)
        r.layer_out[:, half * halfway : (half + 1) * halfway] = total.astype(bf16)

    give(r.gr).wait()

    @pl.when(core == 0)
    def _():
        r.g_sum[...] = (r.gi[...] + r.g_there[...]).astype(bf16)

    @pl.when(core == 1)
    def _():
        r.g_sum[...] = (r.gr[...] + r.g_there[...]).astype(bf16)

    owner = chip + core * (count // 2)

    @pl.when(owner == place)
    def _():
        r.grad_groups[...] = r.g_sum[...]

    @pl.when(owner != place)
    def _():
        links.start(r.g_sum, r.grad_groups, {"tensor": owner}).wait()

    for copy in stored + [bring_block]:
        copy.wait()
    for copy in parts_sent + layers_sent + [w_sent, squares_sent, normed_sent, within_sent]:
        copy.wait_send()
    for gather in (gather_full, gather_normed, gather_matrix):
        gather.close()


def shape(dims, dtype):
    return jax.ShapeDtypeStruct(dims, dtype)


def hand_over(arrays):
    number, most = len(arrays), 512 * 2**10
    pieces = []
    for k, array in enumerate(arrays):
        rows, cols = array.shape
        count = max(1, 2 * rows * cols // most)
        height = rows // count
        pieces += [(k, slice(n * height, (n + 1) * height)) for n in range(count)]

    def body(*refs):
        sources, targets = refs[:number], refs[number : 2 * number]
        held, arrive, leave = refs[2 * number : 3 * number], refs[-2], refs[-1]
        coming, going = [], []
        for n, (k, rows) in enumerate(pieces):
            copy = pltpu.make_async_copy(sources[k].at[rows], held[k].at[rows], arrive.at[n])
            copy.start()
            coming.append(copy)
        for n, (k, rows) in enumerate(pieces):
            coming[n].wait()
            copy = pltpu.make_async_copy(held[k].at[rows], targets[k].at[rows], leave.at[n])
            copy.start()
            going.append(copy)
        for copy in going:
            copy.wait()

    scratch = [pltpu.VMEM(array.shape, array.dtype) for array in arrays]
    scratch += [pltpu.SemaphoreType.DMA((len(pieces),))] * 2
    return pl.pallas_call(
        body,
        out_shape=[shape(array.shape, array.dtype) for array in arrays],
        in_specs=[pl.BlockSpec(memory_space=pltpu.HBM)] * number,
        out_specs=[pl.BlockSpec(memory_space=pltpu.HBM)] * number,
        scratch_shapes=scratch,
        compiler_params=pltpu.CompilerParams(vmem_limit_bytes=62 * 2**20),
    )(*arrays)


def local(
    spread,
    count,
    branch_in,
    gate_in,
    group_proj,
    step_raw,
    conv_inner,
    conv_groups,
    step_bias,
    decay_log,
    skip_gain,
    norm_gain,
    exit_mapping_matrix,
    cotangent,
):
    length, channels = branch_in.shape
    heads = step_raw.shape[1]
    width = exit_mapping_matrix.shape[1]
    operands = dict(
        branch=branch_in,
        gate=gate_in,
        step=step_raw.T,
        conv_inner=conv_inner,
        conv_groups=conv_groups,
        step_bias=step_bias[None],
        decay_log=decay_log[None],
        skip=skip_gain[None],
        gain=norm_gain[None],
        group_proj=group_proj,
        matrix=exit_mapping_matrix,
        cotangent=cotangent,
    )
    results = dict(
        layer_out=shape((length // count, width), bf16),
        grad_branch=shape((length, channels), bf16),
        grad_gate=shape((length, channels), bf16),
        grad_groups=shape((length, STATE), bf16),
        grad_step=shape((heads, length), bf16),
        grad_matrix=shape((channels, width), bf16),
    )
    scratch = work_scratch(length, channels, width, spread, count)
    far = ("group_proj", "matrix", "cotangent", "grad_matrix")

    def spec(name):
        return pl.BlockSpec(memory_space=pl.ANY if name in far else pltpu.VMEM)

    names = list(operands) + list(results) + list(scratch)
    made = pl.pallas_call(
        functools.partial(mixer, names, spread, count),
        out_shape=list(results.values()),
        in_specs=[spec(name) for name in operands],
        out_specs=[spec(name) for name in results],
        scratch_shapes=list(scratch.values()),
        compiler_params=pltpu.CompilerParams(
            collective_id=0, has_side_effects=True, vmem_limit_bytes=62 * 2**20
        ),
    )(*operands.values())
    made = hand_over(made)
    turned = ("grad_step",)
    return tuple(array.T if name in turned else array for name, array in zip(results, made))


def solution(mesh):
    placed = (
        P("dp", "tensor"),
        P("dp", "tensor"),
        P("dp", None),
        P("dp", "tensor"),
        P(None, "tensor"),
        P(),
        P("tensor"),
        P("tensor"),
        P("tensor"),
        P("tensor"),
        P("tensor", None),
        P(("dp", "tensor"), None),
    )
    return jax.shard_map(
        functools.partial(local, mesh.shape["dp"], mesh.shape["tensor"]),
        mesh=mesh,
        in_specs=placed,
        out_specs=(
            P(("dp", "tensor"), None),
            P("dp", "tensor"),
            P("dp", "tensor"),
            P("dp", "tensor"),
            P("dp", "tensor"),
            P("tensor", None),
        ),
        check_vma=False,
    )
```

```python
import functools
from types import SimpleNamespace

import jax
import jax.numpy as jnp
from jax import lax
from jax.experimental import pallas as pl
from jax.experimental.pallas import tpu as pltpu
from jax.sharding import PartitionSpec as P

HEADS = 128
HEAD_DIM = 64
STATE = 256
GROUPS = 8
KERNEL = 4
STRETCH = 128
LANES = 128
f32, bf16 = jnp.float32, jnp.bfloat16
epsilon = 1e-05
NN = (((1,), (0,)), ((), ()))
NT = (((1,), (1,)), ((), ()))
TN = (((0,), (0,)), ((), ()))


def mm(a, b, dims=NN):
    return lax.dot_general(a, b, dims, preferred_element_type=f32)


def mm_exact(a, b, dims=NN):
    return lax.dot_general(a, b, dims, precision=lax.Precision.HIGHEST, preferred_element_type=f32)


def iota(shape, axis):
    return lax.broadcasted_iota(jnp.int32, shape, axis)


def sigmoid(x):
    return 1.0 / (1.0 + jnp.exp(-x))


def later(x, steps):
    return jnp.where(iota(x.shape, 0) >= steps, pltpu.roll(x, steps, 0), 0.0)


def earlier(x, steps):
    length = x.shape[0]
    return jnp.where(iota(x.shape, 0) < length - steps, pltpu.roll(x, length - steps, 0), 0.0)


def conv(x, taps):
    total = taps[KERNEL - 1 : KERNEL] * x
    for steps in range(1, KERNEL):
        total = total + taps[KERNEL - 1 - steps : KERNEL - steps] * later(x, steps)
    return total


def conv_back(g, taps):
    total = taps[KERNEL - 1 : KERNEL] * g
    for steps in range(1, KERNEL):
        total = total + taps[KERNEL - 1 - steps : KERNEL - steps] * earlier(g, steps)
    return total


def silu_slope(x):
    s = sigmoid(x)
    return s * (1.0 + x * (1.0 - s))


def panels(width):
    return [slice(c, c + LANES) for c in range(0, width, LANES)]


def group_taps(r, first, cols):
    start = (first + r.group) * STATE + cols.start
    return r.conv_groups[:, pl.ds(pl.multiple_of(start, LANES), LANES)].astype(f32)


def prepare(r):
    length, channels = r.branch.shape
    heads = r.step.shape[0]
    for cols in panels(channels):
        pre = conv(r.branch[:, cols].astype(f32), r.conv_inner[:, cols].astype(f32))
        r.v[:, cols] = pre * sigmoid(pre)
    for source, first, to in ((r.inp, 0, r.i), (r.ro, GROUPS, r.r)):
        for cols in panels(STATE):
            pre = conv(source[:, cols].astype(f32), group_taps(r, first, cols))
            to[:, cols] = pre * sigmoid(pre)
    small = r.small
    small[...] = jnp.zeros_like(small)
    small[0:1, 0:heads] = r.step_bias[...]
    small[1:2, 0:heads] = -jnp.exp(r.decay_log[...])
    small[2:3, 0:heads] = r.skip[...]
    r.turn[...] = jnp.zeros_like(r.turn)
    r.turn[0:8] = small[...]
    r.small_cols[...] = jnp.transpose(r.turn[...])[0:8]
    square = (STRETCH, STRETCH)
    below = (iota(square, 1) <= iota(square, 0)).astype(f32)
    for k in range(length // STRETCH):
        rows = slice(k * STRETCH, (k + 1) * STRETCH)
        r.turn[0:heads] = r.step[:, rows].astype(f32)
        z = jnp.transpose(r.turn[...]) + small[0:1]
        dt = jnp.maximum(z, 0.0) + jnp.log1p(jnp.exp(-jnp.abs(z)))
        r.dt[rows] = dt
        ld = mm_exact(below, dt * small[1:2])
        r.ld[rows] = ld
        r.ldt[k] = jnp.transpose(ld)[0:8]


def widen(columns, pair):
    first, second = columns[:, 2 * pair : 2 * pair + 1], columns[:, 2 * pair + 1 : 2 * pair + 2]
    low = iota((1, LANES), 1) < HEAD_DIM
    return jnp.where(low, first, second)


def widen_all(row, pairs):
    return jnp.concatenate([widen(row, p) for p in range(pairs)], axis=1)


def split_pair(x):
    low = iota(x.shape, 1) < HEAD_DIM
    zero = jnp.zeros_like(x)
    return jnp.concatenate([jnp.where(low, x, zero), jnp.where(low, zero, x)], axis=0)


def decay_of(ld, ldt, head):
    square = (STRETCH, STRETCH)
    causal = iota(square, 1) <= iota(square, 0)
    spread = ld[:, head : head + 1] - ldt[head : head + 1]
    return jnp.exp(jnp.where(causal, spread, -1e30))


def ssm_forward(r):
    length, channels = r.branch.shape
    pairs = channels // LANES
    prepare(r)
    small = r.small
    r.state[...] = jnp.zeros_like(r.state)

    @pl.loop(0, length // STRETCH)
    def _(k):
        rows = pl.ds(pl.multiple_of(k * STRETCH, STRETCH), STRETCH)
        i_wide, r_wide = r.i[rows], r.r[rows]
        i_now, r_now = i_wide.astype(bf16), r_wide.astype(bf16)
        ld, ldt, dt = r.ld[rows], r.ldt[k], r.dt[rows]
        scores = mm_exact(r_wide, i_wide, NT)
        enter = jnp.exp(ld)
        last = ld[STRETCH - 1 : STRETCH]
        leave = jnp.exp(last - ld)
        held = r.state[...].astype(bf16)
        r.sprev[k] = held
        across = mm(r_now, held)
        carried = []
        squares = jnp.zeros((STRETCH, LANES), f32)
        for p in range(pairs):
            cols = slice(p * LANES, (p + 1) * LANES)
            value = r.v[rows, cols]
            stepped = widen(dt, p) * value
            weights = jnp.concatenate(
                [(scores * decay_of(ld, ldt, 2 * p + h)).astype(bf16) for h in range(2)], axis=1
            )
            y = mm(weights, split_pair(stepped.astype(bf16)))
            y = y + widen(enter, p) * across[:, cols]
            y = y + widen(small[2:3], p) * value
            r.y[rows, cols] = y
            gate = r.gate[rows, cols].astype(f32)
            gated = y * (gate * sigmoid(gate))
            squares = squares + gated * gated
            carried.append((widen(leave, p) * stepped).astype(bf16))
        squares = jnp.sum(squares, axis=1, keepdims=True)
        r.squares[rows] = jnp.broadcast_to(squares, (STRETCH, LANES))
        fresh = mm(i_now, jnp.concatenate(carried, axis=1), TN)
        r.state[...] = widen_all(jnp.exp(last), pairs) * r.state[...] + fresh


def ssm_backward(r):
    length, channels = r.branch.shape
    pairs = channels // LANES
    small = r.small
    r.state[...] = jnp.zeros_like(r.state)
    square = (STRETCH, STRETCH)
    row, col = iota(square, 0), iota(square, 1)
    before = (row < col).astype(bf16)
    before32 = (row < col).astype(f32)
    since32 = (row >= col).astype(f32)
    own = (iota((8, channels), 1) // HEAD_DIM == iota((8, channels), 0)).astype(bf16)

    @pl.loop(0, length // STRETCH)
    def _(turn):
        k = length // STRETCH - 1 - turn
        rows = pl.ds(pl.multiple_of(k * STRETCH, STRETCH), STRETCH)
        i_wide, r_wide = r.i[rows], r.r[rows]
        i_now, r_now = i_wide.astype(bf16), r_wide.astype(bf16)
        ld, ldt, dt = r.ld[rows], r.ldt[k], r.dt[rows]
        scores = mm_exact(r_wide, i_wide, NT)
        enter = jnp.exp(ld)
        last = ld[STRETCH - 1 : STRETCH]
        leave = jnp.exp(last - ld)
        held = r.sprev[k]
        across = mm(r_now, held)
        entering, leaving, crossed, direct, left = [], [], [], [], []
        grad_after = r.state[...].astype(bf16)
        from_state = mm(i_now, grad_after)
        grad_scores = jnp.zeros(square, f32)
        straddle = []
        for p in range(pairs):
            cols = slice(p * LANES, (p + 1) * LANES)
            value = r.v[rows, cols]
            dt_wide = widen(dt, p)
            stepped = dt_wide * value
            gate = r.gate[rows, cols].astype(f32)
            gg = r.gg[rows, cols]
            r.grad_gate[rows, cols] = (gg * r.y[rows, cols] * silu_slope(gate)).astype(bf16)
            gy = gg * (gate * sigmoid(gate))
            gys = split_pair(gy.astype(bf16))
            grad_weights = mm(gys, stepped.astype(bf16), NT)
            weights = []
            for h in range(2):
                decay = decay_of(ld, ldt, 2 * p + h)
                weight = scores * decay
                weights.append(weight.astype(bf16))
                grad_weight = grad_weights[h * STRETCH : (h + 1) * STRETCH]
                grad_scores = grad_scores + grad_weight * decay
                crossing = mm((grad_weight * weight).astype(bf16), before)
                straddle.append(
                    jnp.sum(jnp.where(row >= col, crossing, 0.0), axis=0, keepdims=True)
                )
            grad_stepped = mm(jnp.concatenate(weights, axis=0), gys, TN)
            wide_enter = widen(enter, p) * gy
            entering.append(wide_enter.astype(bf16))
            crossed.append((wide_enter * across[:, cols]).astype(bf16))
            wide_leave = widen(leave, p)
            back = wide_leave * from_state[:, cols]
            grad_stepped = grad_stepped + back
            left.append((back * stepped).astype(bf16))
            leaving.append((wide_leave * stepped).astype(bf16))
            direct.append((grad_stepped * value).astype(bf16))
            r.gv[rows, cols] = dt_wide * grad_stepped + widen(small[2:3], p) * gy
        entering = jnp.concatenate(entering, axis=1)
        gs = grad_scores.astype(bf16)
        r.gr[rows] = mm(gs, i_now) + mm(entering, held, NT)
        grad_in = mm(gs, r_now, TN)
        grad_in = grad_in + mm(jnp.concatenate(leaving, axis=1), grad_after, NT)
        r.gi[rows] = grad_in
        to_heads = lambda parts: mm(own, jnp.concatenate(parts, axis=1), NT)
        grad_x = jnp.concatenate(straddle, axis=0)
        grad_x = grad_x + mm_exact(to_heads(crossed), since32)
        grad_x = grad_x + mm_exact(to_heads(left), before32)
        faded = widen_all(jnp.exp(last), pairs) * r.state[...]
        kept = jnp.sum(faded * held.astype(f32), axis=0, keepdims=True)
        grad_x = grad_x + jnp.sum(own.astype(f32) * kept, axis=1, keepdims=True)
        grad_dt = to_heads(direct) + grad_x * r.small_cols[:, 1:2]
        z = r.step[:, rows].astype(f32) + r.small_cols[:, 0:1]
        r.grad_step[:, rows] = (grad_dt * sigmoid(z)).astype(bf16)
        r.state[...] = faded + mm(r_now, entering, TN)

    for cols in panels(channels):
        taps = r.conv_inner[:, cols].astype(f32)
        pre = conv(r.branch[:, cols].astype(f32), taps)
        r.grad_branch[:, cols] = conv_back(r.gv[:, cols] * silu_slope(pre), taps).astype(bf16)
    for source, first, grad in ((r.inp, 0, r.gi), (r.ro, GROUPS, r.gr)):
        for cols in panels(STATE):
            taps = group_taps(r, first, cols)
            pre = conv(source[:, cols].astype(f32), taps)
            grad[:, cols] = conv_back(grad[:, cols] * silu_slope(pre), taps)


def at_rows(start, count):
    return pl.ds(pl.multiple_of(start, count), count)


class Links:
    def __init__(self, send, receive):
        self.send, self.receive, self.count = send, receive, 0

    def start(self, source, target, device):
        slot = self.count
        self.count += 1
        copy = pltpu.make_async_remote_copy(
            src_ref=source,
            dst_ref=target,
            send_sem=self.send.at[slot],
            recv_sem=self.receive.at[slot],
            device_id=device,
            device_id_type=pl.DeviceIdType.MESH,
        )
        copy.start()
        return copy


class Gather:
    def __init__(self, links, block, pair, ring, devices, own=None, core=None, store=None):
        self.links, self.block, self.pair, self.ring = links, block, pair, ring
        self.to_pair, self.up, self.down = devices
        self.core, self.store = core, store
        self.own = block(pair, ring, None) if own is None else own
        self.sent, self.relays = [], []

    def place(self, other, step, half=None):
        pair = lax.rem(self.pair + other, 2)
        return self.block(pair, lax.rem(self.ring + step + 4, 4), half)

    def go(self, source, target, device):
        self.sent.append(self.links.start(source, target, device))

    def relay(self, source, target):
        if self.core is not None:
            self.relays.append(self.links.start(source, target, self.core))

    def begin(self):
        here = self.place(0, 0)
        for device in (self.to_pair, self.up, self.down):
            self.go(self.own, here, device)
        self.relay(self.own, here)

    def pass_on(self, number):
        self.sent[number].wait_recv()
        if number == 0:
            piece = self.place(1, 0)
            self.go(piece, piece, self.up)
            self.go(piece, piece, self.down)
        elif number <= 4:
            other, upward = (number - 1) // 2, number % 2 == 1
            step, half = (-1, 0) if upward else (1, 1)
            piece = self.place(other, step)
            part = self.place(other, step, half)
            self.go(part, part, self.up if upward else self.down)
        else:
            other, upward = (number - 5) // 2, number % 2 == 1
            piece = self.place(other, 2, 0 if upward else 1)
        self.relay(piece, piece)
        if self.store is not None:
            self.store(*self.arrived(number))

    def arrived(self, number):
        other, upward = (0, True) if number == 0 else ((number - 1) % 4 // 2, number % 2 == 1)
        if number == 0:
            return 1 - self.pair, self.ring
        step = 2 if number > 4 else (-1 if upward else 1)
        pair = lax.rem(self.pair + other, 2)
        half = None if number < 5 else (0 if upward else 1)
        return pair, lax.rem(self.ring + step + 4, 4), half

    def finish(self):
        for copy in self.relays:
            copy.wait_recv()

    def close(self):
        for copy in self.sent + self.relays:
            copy.wait_send()


COPIES = 96
LOCALS = 15


def work_scratch(length, channels, width, spread, count):
    own_rows, part = length // count, width // spread
    halfway = width // 2
    return dict(
        v=pltpu.VMEM((length, channels), f32),
        i=pltpu.VMEM((length, STATE), f32),
        r=pltpu.VMEM((length, STATE), f32),
        dt=pltpu.VMEM((length, LANES), f32),
        ld=pltpu.VMEM((length, LANES), f32),
        ldt=pltpu.VMEM((length // STRETCH, 8, LANES), f32),
        small=pltpu.VMEM((8, LANES), f32),
        state=pltpu.VMEM((STATE, channels), f32),
        sprev=pltpu.VMEM((length // STRETCH, STATE, channels), bf16),
        y=pltpu.VMEM((length, channels), f32),
        squares=pltpu.VMEM((length, LANES), f32),
        squares_there=pltpu.VMEM((length, LANES), f32),
        inv=pltpu.VMEM((length, LANES), f32),
        within=pltpu.VMEM((length, LANES), f32),
        within_there=pltpu.VMEM((length, LANES), f32),
        gv=pltpu.VMEM((length, channels), f32),
        gg=pltpu.VMEM((length, channels), f32),
        gi=pltpu.VMEM((length, STATE), f32),
        gr=pltpu.VMEM((length, STATE), f32),
        g_there=pltpu.VMEM((length, STATE), f32),
        g_sum=pltpu.VMEM((length, STATE), bf16),
        turn=pltpu.VMEM((LANES, LANES), f32),
        small_cols=pltpu.VMEM((8, LANES), f32),
        inp=pltpu.VMEM((length, STATE), bf16),
        ro=pltpu.VMEM((length, STATE), bf16),
        w=pltpu.VMEM((channels, width), bf16),
        w_there=pltpu.VMEM((channels, halfway), bf16),
        normed=pltpu.VMEM((length, channels), bf16),
        normed_there=pltpu.VMEM((length, channels), bf16),
        normed_all=pltpu.VMEM((spread, channels, length), bf16),
        cot_part=pltpu.VMEM((spread, length, part), bf16),
        cot_full=pltpu.VMEM((length, width), bf16),
        product=pltpu.VMEM((channels, part), f32),
        block=pltpu.VMEM((channels, part), bf16),
        layer_part=pltpu.VMEM((length, halfway), bf16),
        layer_there=pltpu.VMEM((count, own_rows, halfway), bf16),
        sends=pltpu.SemaphoreType.DMA((COPIES,)),
        receives=pltpu.SemaphoreType.DMA((COPIES,)),
        ready=pltpu.SemaphoreType.REGULAR,
        local_sems=pltpu.SemaphoreType.DMA((LOCALS,)),
    )


def mixer(names, spread, count, *refs):
    r = SimpleNamespace(**dict(zip(names, refs)))
    length, channels = r.branch.shape
    width = r.matrix.shape[1]
    part, halfway, own_rows = width // spread, width // 2, length // count
    group_span = HEADS * HEAD_DIM // GROUPS
    dp, place = lax.axis_index("dp"), lax.axis_index("tensor")
    core = lax.rem(place, 2)
    other_core = {"tensor": place + 1 - 2 * core}
    r.group = place // 2

    barrier = pltpu.get_barrier_semaphore()
    for k in range(1, spread):
        device = {"dp": lax.rem(dp + k, spread)}
        pl.semaphore_signal(barrier, inc=1, device_id=device, device_id_type=pl.DeviceIdType.MESH)
    for k in range(1, count):
        device = {"tensor": lax.rem(place + k, count)}
        pl.semaphore_signal(barrier, inc=1, device_id=device, device_id_type=pl.DeviceIdType.MESH)

    def bring(source, target, slot):
        copy = pltpu.make_async_copy(source, target, r.local_sems.at[slot])
        copy.start()
        return copy

    input_columns = pl.ds(pl.multiple_of(r.group * STATE, STATE), STATE)
    readout_columns = pl.ds(pl.multiple_of((GROUPS + r.group) * STATE, STATE), STATE)
    bring_in = bring(r.group_proj.at[:, input_columns], r.inp, 0)
    bring_ro = bring(r.group_proj.at[:, readout_columns], r.ro, 1)
    own_part = pl.ds(pl.multiple_of(dp * part, part), part)
    bring_part = bring(
        r.cotangent.at[:, own_part], r.cot_part.at[dp, at_rows(place * own_rows, own_rows)], 2
    )
    bring_full = bring(r.cotangent, r.cot_full.at[at_rows(place * own_rows, own_rows)], 3)
    bring_w = bring(r.matrix, r.w, 4)
    pl.semaphore_wait(barrier, spread + count - 2)

    links = Links(r.sends, r.receives)
    parts_sent = []
    for k in range(1, spread):
        to = lax.rem(dp + k, spread)
        source = r.cotangent.at[:, pl.ds(pl.multiple_of(to * part, part), part)]
        target = r.cot_part.at[dp, at_rows(place * own_rows, own_rows)]
        parts_sent.append(links.start(source, target, {"dp": to}))
    their_half = pl.ds(pl.multiple_of((1 - core) * halfway, halfway), halfway)
    w_sent = links.start(r.matrix.at[:, their_half], r.w_there, other_core)

    bring_in.wait()
    bring_ro.wait()
    ssm_forward(r)
    squares_sent = links.start(r.squares, r.squares_there, other_core)

    chip = place // 2
    column, level = chip // 4, lax.rem(chip, 4)

    def tensor_id(pair, ring):
        return (pair * 4 + ring) * 2 + core

    tensor_devices = [
        {"tensor": tensor_id(1 - column, level)},
        {"tensor": tensor_id(column, lax.rem(level + 1, 4))},
        {"tensor": tensor_id(column, lax.rem(level + 3, 4))},
    ]
    side, depth = dp // 4, lax.rem(dp, 4)
    dp_devices = [
        {"dp": (1 - side) * 4 + depth},
        {"dp": side * 4 + lax.rem(depth + 1, 4)},
        {"dp": side * 4 + lax.rem(depth + 3, 4)},
    ]

    def part_block(pair, ring, half):
        rows = at_rows(tensor_id(pair, ring) * own_rows, own_rows)
        if half is None:
            return r.cot_part.at[:, rows]
        return r.cot_part.at[half * (spread // 2) : (half + 1) * (spread // 2), rows]

    def full_block(pair, ring, half):
        rows = at_rows(tensor_id(pair, ring) * own_rows, own_rows)
        if half is None:
            return r.cot_full.at[rows]
        return r.cot_full.at[rows, half * halfway : (half + 1) * halfway]

    def normed_block(pair, ring, half):
        if half is None:
            return r.normed_all.at[pair * 4 + ring]
        rows = slice(half * (channels // 2), (half + 1) * (channels // 2))
        return r.normed_all.at[pair * 4 + ring, rows]

    def matrix_block(pair, ring, half):
        index = pair * 4 + ring
        if half is None:
            return r.cot_part.at[index]
        return r.cot_part.at[index, half * (channels // 2) : (half + 1) * (channels // 2)]

    stored = []

    def store(pair, ring, half=None):
        cols = pl.ds(pl.multiple_of((pair * 4 + ring) * part, part), part)
        target = r.grad_matrix.at[:, cols]
        if half is not None:
            target = r.grad_matrix.at[half * (channels // 2) : (half + 1) * (channels // 2), cols]
        stored.append(bring(matrix_block(pair, ring, half), target, 5 + len(stored)))

    gather_part = Gather(links, part_block, column, level, tensor_devices, core=other_core)
    gather_full = Gather(
        links, full_block, column, level, tensor_devices, own=r.cotangent, core=other_core
    )
    gather_normed = Gather(links, normed_block, side, depth, dp_devices)
    gather_matrix = Gather(
        links, matrix_block, side, depth, dp_devices, own=r.block, store=store
    )

    bring_part.wait()
    for copy in parts_sent:
        copy.wait_recv()
    gather_part.begin()

    squares_sent.wait_recv()
    r.inv[...] = lax.rsqrt((r.squares[...] + r.squares_there[...]) / group_span + epsilon)
    for cols in panels(channels):
        gate = r.gate[:, cols].astype(f32)
        gated = r.y[:, cols] * (gate * sigmoid(gate))
        normed = gated * r.inv[...] * r.gain[:, cols]
        r.normed[:, cols] = normed.astype(bf16)
        r.normed_all[dp, cols] = jnp.transpose(normed).astype(bf16)
    gather_normed.begin()
    normed_sent = links.start(r.normed, r.normed_there, other_core)

    gather_part.pass_on(0)
    w_sent.wait_recv()
    bring_w.wait()
    normed_sent.wait_recv()
    tile = 256

    @pl.loop(0, halfway // tile)
    def _(step):
        cols = pl.ds(pl.multiple_of(step * tile, tile), tile)
        wide = pl.ds(pl.multiple_of(core * halfway + step * tile, tile), tile)
        total = mm(r.normed[...], r.w[:, wide])
        total = total + mm(r.normed_there[...], r.w_there[:, cols])
        r.layer_part[:, cols] = total.astype(bf16)

    gather_part.pass_on(1)
    gather_part.pass_on(2)
    for number in range(3):
        gather_normed.pass_on(number)
    gather_part.pass_on(3)
    gather_part.pass_on(4)
    gather_normed.pass_on(3)
    gather_normed.pass_on(4)
    gather_full.begin()
    for number in range(5, 9):
        gather_part.pass_on(number)
    gather_part.finish()

    def add_product(index, first=False):
        @pl.loop(0, part // tile)
        def _(step):
            cols = pl.ds(pl.multiple_of(step * tile, tile), tile)
            term = mm(r.normed_all[index], r.cot_part[index, :, cols])
            if first:
                r.product[:, cols] = term
            else:
                r.product[:, cols] += term

    add_product(dp, first=True)
    add_product((1 - side) * 4 + depth)
    for step in (1, 3):
        add_product(side * 4 + lax.rem(depth + step, 4))
        add_product((1 - side) * 4 + lax.rem(depth + step, 4))
    for number in range(5, 9):
        gather_normed.pass_on(number)
    add_product(side * 4 + lax.rem(depth + 2, 4))
    add_product((1 - side) * 4 + lax.rem(depth + 2, 4))
    r.block[...] = r.product[...].astype(bf16)
    gather_part.close()
    for device in dp_devices:
        pl.semaphore_signal(r.ready, inc=1, device_id=device, device_id_type=pl.DeviceIdType.MESH)
    pl.semaphore_wait(r.ready, len(dp_devices))
    gather_matrix.begin()
    own_columns = pl.ds(pl.multiple_of(dp * part, part), part)
    bring_block = bring(r.block, r.grad_matrix.at[:, own_columns], 5 + 9)

    for number in range(5):
        gather_full.pass_on(number)
    layers_sent = []
    column_size = count // 2
    in_column = lax.rem(place, column_size)

    def send_layers(to_column, first):
        for k in range(first, column_size):
            to = to_column * column_size + lax.rem(in_column + k, column_size)
            source = r.layer_part.at[at_rows(to * own_rows, own_rows)]
            layers_sent.append(links.start(source, r.layer_there.at[place], {"tensor": to}))

    send_layers(column, 1)
    gather_matrix.pass_on(0)
    send_layers(1 - column, 0)
    gather_matrix.pass_on(1)
    gather_matrix.pass_on(2)
    for number in range(5, 9):
        gather_full.pass_on(number)
    bring_full.wait()
    gather_full.finish()

    r.gg[...] = jnp.zeros_like(r.gg)
    deep = 512

    @pl.loop(0, width // deep)
    def _(step):
        cols = pl.ds(pl.multiple_of(step * deep, deep), deep)
        r.gg[...] += mm(r.cot_full[:, cols], r.w[:, cols], NT)

    within = jnp.zeros((length, LANES), f32)
    for cols in panels(channels):
        gate = r.gate[:, cols].astype(f32)
        gated = r.y[:, cols] * (gate * sigmoid(gate))
        scaled = r.gain[:, cols] * r.gg[:, cols]
        r.gg[:, cols] = scaled
        within = within + gated * scaled
    within = jnp.sum(within, axis=1, keepdims=True)
    r.within[...] = jnp.broadcast_to(within, (length, LANES))
    within_sent = links.start(r.within, r.within_there, other_core)
    gather_matrix.pass_on(3)
    gather_matrix.pass_on(4)
    within_sent.wait_recv()
    inv = r.inv[...]
    shared = inv * inv * inv * (r.within[...] + r.within_there[...]) * (1.0 / group_span)
    for cols in panels(channels):
        gate = r.gate[:, cols].astype(f32)
        gated = r.y[:, cols] * (gate * sigmoid(gate))
        r.gg[:, cols] = inv * r.gg[:, cols] - gated * shared
    ssm_backward(r)

    given = links.count
    links.count += 1

    def give(source):
        return pltpu.make_async_remote_copy(
            src_ref=source,
            dst_ref=r.g_there,
            send_sem=links.send.at[given],
            recv_sem=links.receive.at[given],
            device_id=other_core,
            device_id_type=pl.DeviceIdType.MESH,
        )

    @pl.when(core == 0)
    def _():
        give(r.gr).start()

    @pl.when(core == 1)
    def _():
        give(r.gi).start()

    for number in range(5, 9):
        gather_matrix.pass_on(number)
    r.layer_there[place] = r.layer_part[at_rows(place * own_rows, own_rows)]
    for copy in layers_sent:
        copy.wait_recv()
    for half in range(2):
        total = r.layer_there[half].astype(f32)
        for source in range(half + 2, count, 2):
            total = total + r.layer_there[source].astype(f32)
        r.layer_out[:, half * halfway : (half + 1) * halfway] = total.astype(bf16)

    give(r.gr).wait()

    @pl.when(core == 0)
    def _():
        r.g_sum[...] = (r.gi[...] + r.g_there[...]).astype(bf16)

    @pl.when(core == 1)
    def _():
        r.g_sum[...] = (r.gr[...] + r.g_there[...]).astype(bf16)

    owner = chip + core * (count // 2)

    @pl.when(owner == place)
    def _():
        r.grad_groups[...] = r.g_sum[...]

    @pl.when(owner != place)
    def _():
        links.start(r.g_sum, r.grad_groups, {"tensor": owner}).wait()

    for copy in stored + [bring_block]:
        copy.wait()
    for copy in parts_sent + layers_sent + [w_sent, squares_sent, normed_sent, within_sent]:
        copy.wait_send()
    for gather in (gather_full, gather_normed, gather_matrix):
        gather.close()


def shape(dims, dtype):
    return jax.ShapeDtypeStruct(dims, dtype)


def hand_over(arrays):
    number, most = len(arrays), 512 * 2**10
    pieces = []
    for k, array in enumerate(arrays):
        rows, cols = array.shape
        count = max(1, 2 * rows * cols // most)
        height = rows // count
        pieces += [(k, slice(n * height, (n + 1) * height)) for n in range(count)]

    def body(*refs):
        sources, targets = refs[:number], refs[number : 2 * number]
        held, arrive, leave = refs[2 * number : 3 * number], refs[-2], refs[-1]
        coming, going = [], []
        for n, (k, rows) in enumerate(pieces):
            copy = pltpu.make_async_copy(sources[k].at[rows], held[k].at[rows], arrive.at[n])
            copy.start()
            coming.append(copy)
        for n, (k, rows) in enumerate(pieces):
            coming[n].wait()
            copy = pltpu.make_async_copy(held[k].at[rows], targets[k].at[rows], leave.at[n])
            copy.start()
            going.append(copy)
        for copy in going:
            copy.wait()

    scratch = [pltpu.VMEM(array.shape, array.dtype) for array in arrays]
    scratch += [pltpu.SemaphoreType.DMA((len(pieces),))] * 2
    return pl.pallas_call(
        body,
        out_shape=[shape(array.shape, array.dtype) for array in arrays],
        in_specs=[pl.BlockSpec(memory_space=pltpu.HBM)] * number,
        out_specs=[pl.BlockSpec(memory_space=pltpu.HBM)] * number,
        scratch_shapes=scratch,
        compiler_params=pltpu.CompilerParams(vmem_limit_bytes=62 * 2**20),
    )(*arrays)


def local(
    spread,
    count,
    branch_in,
    gate_in,
    group_proj,
    step_raw,
    conv_inner,
    conv_groups,
    step_bias,
    decay_log,
    skip_gain,
    norm_gain,
    exit_mapping_matrix,
    cotangent,
):
    length, channels = branch_in.shape
    heads = step_raw.shape[1]
    width = exit_mapping_matrix.shape[1]
    operands = dict(
        branch=branch_in,
        gate=gate_in,
        step=step_raw.T,
        conv_inner=conv_inner,
        conv_groups=conv_groups,
        step_bias=step_bias[None],
        decay_log=decay_log[None],
        skip=skip_gain[None],
        gain=norm_gain[None],
        group_proj=group_proj,
        matrix=exit_mapping_matrix,
        cotangent=cotangent,
    )
    results = dict(
        layer_out=shape((length // count, width), bf16),
        grad_branch=shape((length, channels), bf16),
        grad_gate=shape((length, channels), bf16),
        grad_groups=shape((length, STATE), bf16),
        grad_step=shape((heads, length), bf16),
        grad_matrix=shape((channels, width), bf16),
    )
    scratch = work_scratch(length, channels, width, spread, count)
    far = ("group_proj", "matrix", "cotangent", "grad_matrix")

    def spec(name):
        return pl.BlockSpec(memory_space=pl.ANY if name in far else pltpu.VMEM)

    names = list(operands) + list(results) + list(scratch)
    made = pl.pallas_call(
        functools.partial(mixer, names, spread, count),
        out_shape=list(results.values()),
        in_specs=[spec(name) for name in operands],
        out_specs=[spec(name) for name in results],
        scratch_shapes=list(scratch.values()),
        compiler_params=pltpu.CompilerParams(
            collective_id=0, has_side_effects=True, vmem_limit_bytes=62 * 2**20
        ),
    )(*operands.values())
    made = hand_over(made)
    turned = ("grad_step",)
    return tuple(array.T if name in turned else array for name, array in zip(results, made))


def solution(mesh):
    placed = (
        P("dp", "tensor"),
        P("dp", "tensor"),
        P("dp", None),
        P("dp", "tensor"),
        P(None, "tensor"),
        P(),
        P("tensor"),
        P("tensor"),
        P("tensor"),
        P("tensor"),
        P("tensor", None),
        P(("dp", "tensor"), None),
    )
    return jax.shard_map(
        functools.partial(local, mesh.shape["dp"], mesh.shape["tensor"]),
        mesh=mesh,
        in_specs=placed,
        out_specs=(
            P(("dp", "tensor"), None),
            P("dp", "tensor"),
            P("dp", "tensor"),
            P("dp", "tensor"),
            P("dp", "tensor"),
            P("tensor", None),
        ),
        check_vma=False,
    )
```

```python
import functools
from types import SimpleNamespace

import jax
import jax.numpy as jnp
from jax import lax
from jax.experimental import pallas as pl
from jax.experimental.pallas import tpu as pltpu
from jax.sharding import PartitionSpec as P

HEADS = 128
HEAD_DIM = 64
STATE = 256
GROUPS = 8
KERNEL = 4
STRETCH = 128
LANES = 128
f32, bf16 = jnp.float32, jnp.bfloat16
epsilon = 1e-05
NN = (((1,), (0,)), ((), ()))
NT = (((1,), (1,)), ((), ()))
TN = (((0,), (0,)), ((), ()))


def mm(a, b, dims=NN):
    return lax.dot_general(a, b, dims, preferred_element_type=f32)


def mm_exact(a, b, dims=NN):
    return lax.dot_general(a, b, dims, precision=lax.Precision.HIGHEST, preferred_element_type=f32)


def iota(shape, axis):
    return lax.broadcasted_iota(jnp.int32, shape, axis)


def sigmoid(x):
    return 1.0 / (1.0 + jnp.exp(-x))


def later(x, steps):
    return jnp.where(iota(x.shape, 0) >= steps, pltpu.roll(x, steps, 0), 0.0)


def earlier(x, steps):
    length = x.shape[0]
    return jnp.where(iota(x.shape, 0) < length - steps, pltpu.roll(x, length - steps, 0), 0.0)


def conv(x, taps):
    total = taps[KERNEL - 1 : KERNEL] * x
    for steps in range(1, KERNEL):
        total = total + taps[KERNEL - 1 - steps : KERNEL - steps] * later(x, steps)
    return total


def conv_back(g, taps):
    total = taps[KERNEL - 1 : KERNEL] * g
    for steps in range(1, KERNEL):
        total = total + taps[KERNEL - 1 - steps : KERNEL - steps] * earlier(g, steps)
    return total


def silu_slope(x):
    s = sigmoid(x)
    return s * (1.0 + x * (1.0 - s))


def panels(width):
    return [slice(c, c + LANES) for c in range(0, width, LANES)]


def group_taps(r, first, cols):
    start = (first + r.group) * STATE + cols.start
    return r.conv_groups[:, pl.ds(pl.multiple_of(start, LANES), LANES)].astype(f32)


def prepare(r):
    length, channels = r.branch.shape
    heads = r.step.shape[0]
    for cols in panels(channels):
        pre = conv(r.branch[:, cols].astype(f32), r.conv_inner[:, cols].astype(f32))
        r.v[:, cols] = pre * sigmoid(pre)
    for source, first, to in ((r.inp, 0, r.i), (r.ro, GROUPS, r.r)):
        for cols in panels(STATE):
            pre = conv(source[:, cols].astype(f32), group_taps(r, first, cols))
            to[:, cols] = pre * sigmoid(pre)
    small = r.small
    small[...] = jnp.zeros_like(small)
    small[0:1, 0:heads] = r.step_bias[...]
    small[1:2, 0:heads] = -jnp.exp(r.decay_log[...])
    small[2:3, 0:heads] = r.skip[...]
    r.turn[...] = jnp.zeros_like(r.turn)
    r.turn[0:8] = small[...]
    r.small_cols[...] = jnp.transpose(r.turn[...])[0:8]
    square = (STRETCH, STRETCH)
    below = (iota(square, 1) <= iota(square, 0)).astype(f32)
    for k in range(length // STRETCH):
        rows = slice(k * STRETCH, (k + 1) * STRETCH)
        r.turn[0:heads] = r.step[:, rows].astype(f32)
        z = jnp.transpose(r.turn[...]) + small[0:1]
        dt = jnp.maximum(z, 0.0) + jnp.log1p(jnp.exp(-jnp.abs(z)))
        r.dt[rows] = dt
        ld = mm_exact(below, dt * small[1:2])
        r.ld[rows] = ld
        r.ldt[k] = jnp.transpose(ld)[0:8]


def widen(columns, pair):
    first, second = columns[:, 2 * pair : 2 * pair + 1], columns[:, 2 * pair + 1 : 2 * pair + 2]
    low = iota((1, LANES), 1) < HEAD_DIM
    return jnp.where(low, first, second)


def widen_all(row, pairs):
    return jnp.concatenate([widen(row, p) for p in range(pairs)], axis=1)


def split_pair(x):
    low = iota(x.shape, 1) < HEAD_DIM
    zero = jnp.zeros_like(x)
    return jnp.concatenate([jnp.where(low, x, zero), jnp.where(low, zero, x)], axis=0)


def decay_of(ld, ldt, head):
    square = (STRETCH, STRETCH)
    causal = iota(square, 1) <= iota(square, 0)
    spread = ld[:, head : head + 1] - ldt[head : head + 1]
    return jnp.exp(jnp.where(causal, spread, -1e30))


def ssm_forward(r):
    length, channels = r.branch.shape
    pairs = channels // LANES
    prepare(r)
    small = r.small
    r.state[...] = jnp.zeros_like(r.state)

    @pl.loop(0, length // STRETCH)
    def _(k):
        rows = pl.ds(pl.multiple_of(k * STRETCH, STRETCH), STRETCH)
        i_wide, r_wide = r.i[rows], r.r[rows]
        i_now, r_now = i_wide.astype(bf16), r_wide.astype(bf16)
        ld, ldt, dt = r.ld[rows], r.ldt[k], r.dt[rows]
        scores = mm_exact(r_wide, i_wide, NT)
        enter = jnp.exp(ld)
        last = ld[STRETCH - 1 : STRETCH]
        leave = jnp.exp(last - ld)
        held = r.state[...].astype(bf16)
        r.sprev[k] = held
        across = mm(r_now, held)
        carried = []
        squares = jnp.zeros((STRETCH, LANES), f32)
        for p in range(pairs):
            cols = slice(p * LANES, (p + 1) * LANES)
            value = r.v[rows, cols]
            stepped = widen(dt, p) * value
            weights = jnp.concatenate(
                [(scores * decay_of(ld, ldt, 2 * p + h)).astype(bf16) for h in range(2)], axis=1
            )
            y = mm(weights, split_pair(stepped.astype(bf16)))
            y = y + widen(enter, p) * across[:, cols]
            y = y + widen(small[2:3], p) * value
            r.y[rows, cols] = y
            gate = r.gate[rows, cols].astype(f32)
            gated = y * (gate * sigmoid(gate))
            squares = squares + gated * gated
            carried.append((widen(leave, p) * stepped).astype(bf16))
        squares = jnp.sum(squares, axis=1, keepdims=True)
        r.squares[rows] = jnp.broadcast_to(squares, (STRETCH, LANES))
        fresh = mm(i_now, jnp.concatenate(carried, axis=1), TN)
        r.state[...] = widen_all(jnp.exp(last), pairs) * r.state[...] + fresh


def ssm_backward(r):
    length, channels = r.branch.shape
    pairs = channels // LANES
    small = r.small
    r.state[...] = jnp.zeros_like(r.state)
    square = (STRETCH, STRETCH)
    row, col = iota(square, 0), iota(square, 1)
    before = (row < col).astype(bf16)
    before32 = (row < col).astype(f32)
    since32 = (row >= col).astype(f32)
    own = (iota((8, channels), 1) // HEAD_DIM == iota((8, channels), 0)).astype(bf16)

    @pl.loop(0, length // STRETCH)
    def _(turn):
        k = length // STRETCH - 1 - turn
        rows = pl.ds(pl.multiple_of(k * STRETCH, STRETCH), STRETCH)
        i_wide, r_wide = r.i[rows], r.r[rows]
        i_now, r_now = i_wide.astype(bf16), r_wide.astype(bf16)
        ld, ldt, dt = r.ld[rows], r.ldt[k], r.dt[rows]
        scores = mm_exact(r_wide, i_wide, NT)
        enter = jnp.exp(ld)
        last = ld[STRETCH - 1 : STRETCH]
        leave = jnp.exp(last - ld)
        held = r.sprev[k]
        across = mm(r_now, held)
        entering, leaving, crossed, direct, left = [], [], [], [], []
        grad_after = r.state[...].astype(bf16)
        from_state = mm(i_now, grad_after)
        grad_scores = jnp.zeros(square, f32)
        straddle = []
        for p in range(pairs):
            cols = slice(p * LANES, (p + 1) * LANES)
            value = r.v[rows, cols]
            dt_wide = widen(dt, p)
            stepped = dt_wide * value
            gate = r.gate[rows, cols].astype(f32)
            gg = r.gg[rows, cols]
            r.grad_gate[rows, cols] = (gg * r.y[rows, cols] * silu_slope(gate)).astype(bf16)
            gy = gg * (gate * sigmoid(gate))
            gys = split_pair(gy.astype(bf16))
            grad_weights = mm(gys, stepped.astype(bf16), NT)
            weights = []
            for h in range(2):
                decay = decay_of(ld, ldt, 2 * p + h)
                weight = scores * decay
                weights.append(weight.astype(bf16))
                grad_weight = grad_weights[h * STRETCH : (h + 1) * STRETCH]
                grad_scores = grad_scores + grad_weight * decay
                crossing = mm((grad_weight * weight).astype(bf16), before)
                straddle.append(
                    jnp.sum(jnp.where(row >= col, crossing, 0.0), axis=0, keepdims=True)
                )
            grad_stepped = mm(jnp.concatenate(weights, axis=0), gys, TN)
            wide_enter = widen(enter, p) * gy
            entering.append(wide_enter.astype(bf16))
            crossed.append((wide_enter * across[:, cols]).astype(bf16))
            wide_leave = widen(leave, p)
            back = wide_leave * from_state[:, cols]
            grad_stepped = grad_stepped + back
            left.append((back * stepped).astype(bf16))
            leaving.append((wide_leave * stepped).astype(bf16))
            direct.append((grad_stepped * value).astype(bf16))
            r.gv[rows, cols] = dt_wide * grad_stepped + widen(small[2:3], p) * gy
        entering = jnp.concatenate(entering, axis=1)
        gs = grad_scores.astype(bf16)
        r.gr[rows] = mm(gs, i_now) + mm(entering, held, NT)
        grad_in = mm(gs, r_now, TN)
        grad_in = grad_in + mm(jnp.concatenate(leaving, axis=1), grad_after, NT)
        r.gi[rows] = grad_in
        to_heads = lambda parts: mm(own, jnp.concatenate(parts, axis=1), NT)
        grad_x = jnp.concatenate(straddle, axis=0)
        grad_x = grad_x + mm_exact(to_heads(crossed), since32)
        grad_x = grad_x + mm_exact(to_heads(left), before32)
        faded = widen_all(jnp.exp(last), pairs) * r.state[...]
        kept = jnp.sum(faded * held.astype(f32), axis=0, keepdims=True)
        grad_x = grad_x + jnp.sum(own.astype(f32) * kept, axis=1, keepdims=True)
        grad_dt = to_heads(direct) + grad_x * r.small_cols[:, 1:2]
        z = r.step[:, rows].astype(f32) + r.small_cols[:, 0:1]
        r.grad_step[:, rows] = (grad_dt * sigmoid(z)).astype(bf16)
        r.state[...] = faded + mm(r_now, entering, TN)

    for cols in panels(channels):
        taps = r.conv_inner[:, cols].astype(f32)
        pre = conv(r.branch[:, cols].astype(f32), taps)
        r.grad_branch[:, cols] = conv_back(r.gv[:, cols] * silu_slope(pre), taps).astype(bf16)
    for source, first, grad in ((r.inp, 0, r.gi), (r.ro, GROUPS, r.gr)):
        for cols in panels(STATE):
            taps = group_taps(r, first, cols)
            pre = conv(source[:, cols].astype(f32), taps)
            grad[:, cols] = conv_back(grad[:, cols] * silu_slope(pre), taps)


def at_rows(start, count):
    return pl.ds(pl.multiple_of(start, count), count)


class Links:
    def __init__(self, send, receive):
        self.send, self.receive, self.count = send, receive, 0

    def start(self, source, target, device):
        slot = self.count
        self.count += 1
        copy = pltpu.make_async_remote_copy(
            src_ref=source,
            dst_ref=target,
            send_sem=self.send.at[slot],
            recv_sem=self.receive.at[slot],
            device_id=device,
            device_id_type=pl.DeviceIdType.MESH,
        )
        copy.start()
        return copy


class Gather:
    def __init__(self, links, block, pair, ring, devices, own=None, core=None, store=None):
        self.links, self.block, self.pair, self.ring = links, block, pair, ring
        self.to_pair, self.up, self.down = devices
        self.core, self.store = core, store
        self.own = block(pair, ring, None) if own is None else own
        self.sent, self.relays = [], []

    def place(self, other, step, half=None):
        pair = lax.rem(self.pair + other, 2)
        return self.block(pair, lax.rem(self.ring + step + 4, 4), half)

    def go(self, source, target, device):
        self.sent.append(self.links.start(source, target, device))

    def relay(self, source, target):
        if self.core is not None:
            self.relays.append(self.links.start(source, target, self.core))

    def begin(self):
        here = self.place(0, 0)
        for device in (self.to_pair, self.up, self.down):
            self.go(self.own, here, device)
        self.relay(self.own, here)

    def pass_on(self, number):
        self.sent[number].wait_recv()
        if number == 0:
            piece = self.place(1, 0)
            self.go(piece, piece, self.up)
            self.go(piece, piece, self.down)
        elif number <= 4:
            other, upward = (number - 1) // 2, number % 2 == 1
            step, half = (-1, 0) if upward else (1, 1)
            piece = self.place(other, step)
            part = self.place(other, step, half)
            self.go(part, part, self.up if upward else self.down)
        else:
            other, upward = (number - 5) // 2, number % 2 == 1
            piece = self.place(other, 2, 0 if upward else 1)
        self.relay(piece, piece)
        if self.store is not None:
            self.store(*self.arrived(number))

    def arrived(self, number):
        other, upward = (0, True) if number == 0 else ((number - 1) % 4 // 2, number % 2 == 1)
        if number == 0:
            return 1 - self.pair, self.ring
        step = 2 if number > 4 else (-1 if upward else 1)
        pair = lax.rem(self.pair + other, 2)
        half = None if number < 5 else (0 if upward else 1)
        return pair, lax.rem(self.ring + step + 4, 4), half

    def finish(self):
        for copy in self.relays:
            copy.wait_recv()

    def close(self):
        for copy in self.sent + self.relays:
            copy.wait_send()


COPIES = 96
LOCALS = 15


def work_scratch(length, channels, width, spread, count):
    own_rows, part = length // count, width // spread
    halfway = width // 2
    return dict(
        v=pltpu.VMEM((length, channels), f32),
        i=pltpu.VMEM((length, STATE), f32),
        r=pltpu.VMEM((length, STATE), f32),
        dt=pltpu.VMEM((length, LANES), f32),
        ld=pltpu.VMEM((length, LANES), f32),
        ldt=pltpu.VMEM((length // STRETCH, 8, LANES), f32),
        small=pltpu.VMEM((8, LANES), f32),
        state=pltpu.VMEM((STATE, channels), f32),
        sprev=pltpu.VMEM((length // STRETCH, STATE, channels), bf16),
        y=pltpu.VMEM((length, channels), f32),
        squares=pltpu.VMEM((length, LANES), f32),
        squares_there=pltpu.VMEM((length, LANES), f32),
        inv=pltpu.VMEM((length, LANES), f32),
        within=pltpu.VMEM((length, LANES), f32),
        within_there=pltpu.VMEM((length, LANES), f32),
        gv=pltpu.VMEM((length, channels), f32),
        gg=pltpu.VMEM((length, channels), f32),
        gi=pltpu.VMEM((length, STATE), f32),
        gr=pltpu.VMEM((length, STATE), f32),
        g_there=pltpu.VMEM((length, STATE), f32),
        g_sum=pltpu.VMEM((length, STATE), bf16),
        turn=pltpu.VMEM((LANES, LANES), f32),
        small_cols=pltpu.VMEM((8, LANES), f32),
        inp=pltpu.VMEM((length, STATE), bf16),
        ro=pltpu.VMEM((length, STATE), bf16),
        w=pltpu.VMEM((channels, width), bf16),
        w_there=pltpu.VMEM((channels, halfway), bf16),
        normed=pltpu.VMEM((length, channels), bf16),
        normed_there=pltpu.VMEM((length, channels), bf16),
        normed_all=pltpu.VMEM((spread, channels, length), bf16),
        cot_part=pltpu.VMEM((spread, length, part), bf16),
        cot_full=pltpu.VMEM((length, width), bf16),
        product=pltpu.VMEM((channels, part), f32),
        block=pltpu.VMEM((channels, part), bf16),
        layer_part=pltpu.VMEM((length, halfway), bf16),
        layer_there=pltpu.VMEM((count, own_rows, halfway), bf16),
        sends=pltpu.SemaphoreType.DMA((COPIES,)),
        receives=pltpu.SemaphoreType.DMA((COPIES,)),
        ready=pltpu.SemaphoreType.REGULAR,
        local_sems=pltpu.SemaphoreType.DMA((LOCALS,)),
    )


def mixer(names, spread, count, *refs):
    r = SimpleNamespace(**dict(zip(names, refs)))
    length, channels = r.branch.shape
    width = r.matrix.shape[1]
    part, halfway, own_rows = width // spread, width // 2, length // count
    group_span = HEADS * HEAD_DIM // GROUPS
    dp, place = lax.axis_index("dp"), lax.axis_index("tensor")
    core = lax.rem(place, 2)
    other_core = {"tensor": place + 1 - 2 * core}
    r.group = place // 2

    barrier = pltpu.get_barrier_semaphore()
    for k in range(1, spread):
        device = {"dp": lax.rem(dp + k, spread)}
        pl.semaphore_signal(barrier, inc=1, device_id=device, device_id_type=pl.DeviceIdType.MESH)
    for k in range(1, count):
        device = {"tensor": lax.rem(place + k, count)}
        pl.semaphore_signal(barrier, inc=1, device_id=device, device_id_type=pl.DeviceIdType.MESH)

    def bring(source, target, slot):
        copy = pltpu.make_async_copy(source, target, r.local_sems.at[slot])
        copy.start()
        return copy

    input_columns = pl.ds(pl.multiple_of(r.group * STATE, STATE), STATE)
    readout_columns = pl.ds(pl.multiple_of((GROUPS + r.group) * STATE, STATE), STATE)
    bring_in = bring(r.group_proj.at[:, input_columns], r.inp, 0)
    bring_ro = bring(r.group_proj.at[:, readout_columns], r.ro, 1)
    own_part = pl.ds(pl.multiple_of(dp * part, part), part)
    bring_part = bring(
        r.cotangent.at[:, own_part], r.cot_part.at[dp, at_rows(place * own_rows, own_rows)], 2
    )
    bring_full = bring(r.cotangent, r.cot_full.at[at_rows(place * own_rows, own_rows)], 3)
    bring_w = bring(r.matrix, r.w, 4)
    pl.semaphore_wait(barrier, spread + count - 2)

    links = Links(r.sends, r.receives)
    parts_sent = []
    for k in range(1, spread):
        to = lax.rem(dp + k, spread)
        source = r.cotangent.at[:, pl.ds(pl.multiple_of(to * part, part), part)]
        target = r.cot_part.at[dp, at_rows(place * own_rows, own_rows)]
        parts_sent.append(links.start(source, target, {"dp": to}))
    their_half = pl.ds(pl.multiple_of((1 - core) * halfway, halfway), halfway)
    w_sent = links.start(r.matrix.at[:, their_half], r.w_there, other_core)

    bring_in.wait()
    bring_ro.wait()
    ssm_forward(r)
    squares_sent = links.start(r.squares, r.squares_there, other_core)

    chip = place // 2
    column, level = chip // 4, lax.rem(chip, 4)

    def tensor_id(pair, ring):
        return (pair * 4 + ring) * 2 + core

    tensor_devices = [
        {"tensor": tensor_id(1 - column, level)},
        {"tensor": tensor_id(column, lax.rem(level + 1, 4))},
        {"tensor": tensor_id(column, lax.rem(level + 3, 4))},
    ]
    side, depth = dp // 4, lax.rem(dp, 4)
    dp_devices = [
        {"dp": (1 - side) * 4 + depth},
        {"dp": side * 4 + lax.rem(depth + 1, 4)},
        {"dp": side * 4 + lax.rem(depth + 3, 4)},
    ]

    def part_block(pair, ring, half):
        rows = at_rows(tensor_id(pair, ring) * own_rows, own_rows)
        if half is None:
            return r.cot_part.at[:, rows]
        return r.cot_part.at[half * (spread // 2) : (half + 1) * (spread // 2), rows]

    def full_block(pair, ring, half):
        rows = at_rows(tensor_id(pair, ring) * own_rows, own_rows)
        if half is None:
            return r.cot_full.at[rows]
        return r.cot_full.at[rows, half * halfway : (half + 1) * halfway]

    def normed_block(pair, ring, half):
        if half is None:
            return r.normed_all.at[pair * 4 + ring]
        rows = slice(half * (channels // 2), (half + 1) * (channels // 2))
        return r.normed_all.at[pair * 4 + ring, rows]

    def matrix_block(pair, ring, half):
        index = pair * 4 + ring
        if half is None:
            return r.cot_part.at[index]
        return r.cot_part.at[index, half * (channels // 2) : (half + 1) * (channels // 2)]

    stored = []

    def store(pair, ring, half=None):
        cols = pl.ds(pl.multiple_of((pair * 4 + ring) * part, part), part)
        target = r.grad_matrix.at[:, cols]
        if half is not None:
            target = r.grad_matrix.at[half * (channels // 2) : (half + 1) * (channels // 2), cols]
        stored.append(bring(matrix_block(pair, ring, half), target, 5 + len(stored)))

    gather_part = Gather(links, part_block, column, level, tensor_devices, core=other_core)
    gather_full = Gather(
        links, full_block, column, level, tensor_devices, own=r.cotangent, core=other_core
    )
    gather_normed = Gather(links, normed_block, side, depth, dp_devices)
    gather_matrix = Gather(
        links, matrix_block, side, depth, dp_devices, own=r.block, store=store
    )

    bring_part.wait()
    for copy in parts_sent:
        copy.wait_recv()
    gather_part.begin()

    squares_sent.wait_recv()
    r.inv[...] = lax.rsqrt((r.squares[...] + r.squares_there[...]) / group_span + epsilon)
    for cols in panels(channels):
        gate = r.gate[:, cols].astype(f32)
        gated = r.y[:, cols] * (gate * sigmoid(gate))
        normed = gated * r.inv[...] * r.gain[:, cols]
        r.normed[:, cols] = normed.astype(bf16)
        r.normed_all[dp, cols] = jnp.transpose(normed).astype(bf16)
    gather_normed.begin()
    normed_sent = links.start(r.normed, r.normed_there, other_core)

    gather_part.pass_on(0)
    w_sent.wait_recv()
    bring_w.wait()
    normed_sent.wait_recv()
    tile = 256

    @pl.loop(0, halfway // tile)
    def _(step):
        cols = pl.ds(pl.multiple_of(step * tile, tile), tile)
        wide = pl.ds(pl.multiple_of(core * halfway + step * tile, tile), tile)
        total = mm(r.normed[...], r.w[:, wide])
        total = total + mm(r.normed_there[...], r.w_there[:, cols])
        r.layer_part[:, cols] = total.astype(bf16)

    gather_part.pass_on(1)
    gather_part.pass_on(2)
    for number in range(3):
        gather_normed.pass_on(number)
    gather_part.pass_on(3)
    gather_part.pass_on(4)
    gather_normed.pass_on(3)
    gather_normed.pass_on(4)
    gather_full.begin()
    for number in range(5, 9):
        gather_part.pass_on(number)
    gather_part.finish()

    def add_product(index, first=False):
        @pl.loop(0, part // tile)
        def _(step):
            cols = pl.ds(pl.multiple_of(step * tile, tile), tile)
            term = mm(r.normed_all[index], r.cot_part[index, :, cols])
            if first:
                r.product[:, cols] = term
            else:
                r.product[:, cols] += term

    add_product(dp, first=True)
    add_product((1 - side) * 4 + depth)
    for step in (1, 3):
        add_product(side * 4 + lax.rem(depth + step, 4))
        add_product((1 - side) * 4 + lax.rem(depth + step, 4))
    for number in range(5, 9):
        gather_normed.pass_on(number)
    add_product(side * 4 + lax.rem(depth + 2, 4))
    add_product((1 - side) * 4 + lax.rem(depth + 2, 4))
    r.block[...] = r.product[...].astype(bf16)
    gather_part.close()
    for device in dp_devices:
        pl.semaphore_signal(r.ready, inc=1, device_id=device, device_id_type=pl.DeviceIdType.MESH)
    pl.semaphore_wait(r.ready, len(dp_devices))
    gather_matrix.begin()
    own_columns = pl.ds(pl.multiple_of(dp * part, part), part)
    bring_block = bring(r.block, r.grad_matrix.at[:, own_columns], 5 + 9)

    for number in range(5):
        gather_full.pass_on(number)
    layers_sent = []
    column_size = count // 2
    in_column = lax.rem(place, column_size)

    def send_layers(to_column, first):
        for k in range(first, column_size):
            to = to_column * column_size + lax.rem(in_column + k, column_size)
            source = r.layer_part.at[at_rows(to * own_rows, own_rows)]
            layers_sent.append(links.start(source, r.layer_there.at[place], {"tensor": to}))

    send_layers(column, 1)
    gather_matrix.pass_on(0)
    send_layers(1 - column, 0)
    gather_matrix.pass_on(1)
    gather_matrix.pass_on(2)
    for number in range(5, 9):
        gather_full.pass_on(number)
    bring_full.wait()
    gather_full.finish()

    r.gg[...] = jnp.zeros_like(r.gg)
    deep = 512

    @pl.loop(0, width // deep)
    def _(step):
        cols = pl.ds(pl.multiple_of(step * deep, deep), deep)
        r.gg[...] += mm(r.cot_full[:, cols], r.w[:, cols], NT)

    within = jnp.zeros((length, LANES), f32)
    for cols in panels(channels):
        gate = r.gate[:, cols].astype(f32)
        gated = r.y[:, cols] * (gate * sigmoid(gate))
        scaled = r.gain[:, cols] * r.gg[:, cols]
        r.gg[:, cols] = scaled
        within = within + gated * scaled
    within = jnp.sum(within, axis=1, keepdims=True)
    r.within[...] = jnp.broadcast_to(within, (length, LANES))
    within_sent = links.start(r.within, r.within_there, other_core)
    gather_matrix.pass_on(3)
    gather_matrix.pass_on(4)
    within_sent.wait_recv()
    inv = r.inv[...]
    shared = inv * inv * inv * (r.within[...] + r.within_there[...]) * (1.0 / group_span)
    for cols in panels(channels):
        gate = r.gate[:, cols].astype(f32)
        gated = r.y[:, cols] * (gate * sigmoid(gate))
        r.gg[:, cols] = inv * r.gg[:, cols] - gated * shared
    ssm_backward(r)

    given = links.count
    links.count += 1

    def give(source):
        return pltpu.make_async_remote_copy(
            src_ref=source,
            dst_ref=r.g_there,
            send_sem=links.send.at[given],
            recv_sem=links.receive.at[given],
            device_id=other_core,
            device_id_type=pl.DeviceIdType.MESH,
        )

    @pl.when(core == 0)
    def _():
        give(r.gr).start()

    @pl.when(core == 1)
    def _():
        give(r.gi).start()

    give(r.gr).wait()

    @pl.when(core == 0)
    def _():
        r.g_sum[...] = (r.gi[...] + r.g_there[...]).astype(bf16)

    @pl.when(core == 1)
    def _():
        r.g_sum[...] = (r.gr[...] + r.g_there[...]).astype(bf16)

    owner = chip + core * (count // 2)

    @pl.when(owner == place)
    def _():
        r.grad_groups[...] = r.g_sum[...]

    @pl.when(owner != place)
    def _():
        links.start(r.g_sum, r.grad_groups, {"tensor": owner}).wait()

    r.layer_there[place] = r.layer_part[at_rows(place * own_rows, own_rows)]
    for copy in layers_sent:
        copy.wait_recv()
    for half in range(2):
        total = r.layer_there[half].astype(f32)
        for source in range(half + 2, count, 2):
            total = total + r.layer_there[source].astype(f32)
        r.layer_out[:, half * halfway : (half + 1) * halfway] = total.astype(bf16)

    for number in range(5, 9):
        gather_matrix.pass_on(number)
    for copy in stored + [bring_block]:
        copy.wait()
    for copy in parts_sent + layers_sent + [w_sent, squares_sent, normed_sent, within_sent]:
        copy.wait_send()
    for gather in (gather_full, gather_normed, gather_matrix):
        gather.close()


def shape(dims, dtype):
    return jax.ShapeDtypeStruct(dims, dtype)


def hand_over(arrays):
    number, most = len(arrays), 512 * 2**10
    pieces = []
    for k, array in enumerate(arrays):
        rows, cols = array.shape
        count = max(1, 2 * rows * cols // most)
        height = rows // count
        pieces += [(k, slice(n * height, (n + 1) * height)) for n in range(count)]

    def body(*refs):
        sources, targets = refs[:number], refs[number : 2 * number]
        held, arrive, leave = refs[2 * number : 3 * number], refs[-2], refs[-1]
        coming, going = [], []
        for n, (k, rows) in enumerate(pieces):
            copy = pltpu.make_async_copy(sources[k].at[rows], held[k].at[rows], arrive.at[n])
            copy.start()
            coming.append(copy)
        for n, (k, rows) in enumerate(pieces):
            coming[n].wait()
            copy = pltpu.make_async_copy(held[k].at[rows], targets[k].at[rows], leave.at[n])
            copy.start()
            going.append(copy)
        for copy in going:
            copy.wait()

    scratch = [pltpu.VMEM(array.shape, array.dtype) for array in arrays]
    scratch += [pltpu.SemaphoreType.DMA((len(pieces),))] * 2
    return pl.pallas_call(
        body,
        out_shape=[shape(array.shape, array.dtype) for array in arrays],
        in_specs=[pl.BlockSpec(memory_space=pltpu.HBM)] * number,
        out_specs=[pl.BlockSpec(memory_space=pltpu.HBM)] * number,
        scratch_shapes=scratch,
        compiler_params=pltpu.CompilerParams(vmem_limit_bytes=62 * 2**20),
    )(*arrays)


def local(
    spread,
    count,
    branch_in,
    gate_in,
    group_proj,
    step_raw,
    conv_inner,
    conv_groups,
    step_bias,
    decay_log,
    skip_gain,
    norm_gain,
    exit_mapping_matrix,
    cotangent,
):
    length, channels = branch_in.shape
    heads = step_raw.shape[1]
    width = exit_mapping_matrix.shape[1]
    operands = dict(
        branch=branch_in,
        gate=gate_in,
        step=step_raw.T,
        conv_inner=conv_inner,
        conv_groups=conv_groups,
        step_bias=step_bias[None],
        decay_log=decay_log[None],
        skip=skip_gain[None],
        gain=norm_gain[None],
        group_proj=group_proj,
        matrix=exit_mapping_matrix,
        cotangent=cotangent,
    )
    results = dict(
        layer_out=shape((length // count, width), bf16),
        grad_branch=shape((length, channels), bf16),
        grad_gate=shape((length, channels), bf16),
        grad_groups=shape((length, STATE), bf16),
        grad_step=shape((heads, length), bf16),
        grad_matrix=shape((channels, width), bf16),
    )
    scratch = work_scratch(length, channels, width, spread, count)
    far = ("group_proj", "matrix", "cotangent", "grad_matrix")

    def spec(name):
        return pl.BlockSpec(memory_space=pl.ANY if name in far else pltpu.VMEM)

    names = list(operands) + list(results) + list(scratch)
    made = pl.pallas_call(
        functools.partial(mixer, names, spread, count),
        out_shape=list(results.values()),
        in_specs=[spec(name) for name in operands],
        out_specs=[spec(name) for name in results],
        scratch_shapes=list(scratch.values()),
        compiler_params=pltpu.CompilerParams(
            collective_id=0, has_side_effects=True, vmem_limit_bytes=62 * 2**20
        ),
    )(*operands.values())
    made = hand_over(made)
    turned = ("grad_step",)
    return tuple(array.T if name in turned else array for name, array in zip(results, made))


def solution(mesh):
    placed = (
        P("dp", "tensor"),
        P("dp", "tensor"),
        P("dp", None),
        P("dp", "tensor"),
        P(None, "tensor"),
        P(),
        P("tensor"),
        P("tensor"),
        P("tensor"),
        P("tensor"),
        P("tensor", None),
        P(("dp", "tensor"), None),
    )
    return jax.shard_map(
        functools.partial(local, mesh.shape["dp"], mesh.shape["tensor"]),
        mesh=mesh,
        in_specs=placed,
        out_specs=(
            P(("dp", "tensor"), None),
            P("dp", "tensor"),
            P("dp", "tensor"),
            P("dp", "tensor"),
            P("dp", "tensor"),
            P("tensor", None),
        ),
        check_vma=False,
    )
```
